32 devices in a mesh: dp: 4 (over y, core), expert: 8 (over z, x).
Axes of the slice: x: 2, y: 2, z: 4, core: 2. Of those that a mesh axis runs over, the one named last changes fastest.
Arguments:
- tokens: bfloat16 [4096, 4096], P(('dp', 'expert')), may hold values from -6 to 6
- out_grad: bfloat16 [4096, 4096], P(('dp', 'expert')), may hold values from -0.29882812 to 0.29882812
- probs: bfloat16 [4096, 8], P(('dp', 'expert')), may hold values from 0.049804688 to 0.5
- routes: int32 [4096, 8], P(('dp', 'expert')), may hold values from 0 to 31, as said below
- saved_gate: bfloat16 [16384, 768], P(('dp', 'expert')), may hold values from -6 to 6
- saved_up: bfloat16 [16384, 768], P(('dp', 'expert')), may hold values from -6 to 6
- down_weight: bfloat16 [8, 768, 4096], P('expert'), may hold values from -0.21875 to 0.21875
Outputs:
- grad_down: float32 [8, 768, 4096], P('expert', 'dp')
- grad_up: bfloat16 [8, 4096, 768], P('expert', 'dp')
- prob_grad: float32 [4096, 8], P(('dp', 'expert'))
The draws below stay inside these ranges and needn't reach their ends.
Inputs may be any that keep to these rules, and one draw needn't show every extreme that they name: `routes`: each row names 8 different experts. In every aligned block of 128 rows at least half of the rows name one common expert whose number is a multiple of 4; which one is drawn from the seed.
All inputs are finite; a program needn't handle non-finite values.
Results may differ from the reference program's by a relative error of at most 0.014.
Values may be sent and summed in bfloat16 or wider, within the bound.
No kernel may reach another device: no remote copies, remote signals or barrier semaphores. Data moves between devices by JAX's collectives and lax.ppermute only.
A program may use at most 192 MiB of HBM per device.

```python
import jax
import jax.numpy as jnp
from jax import lax

D = 4096
FF = 768
TOP = 8
EXP_DEV = 4
TOK_DEV = 128
EXPERTS = 32
WINDOW = 8
CAP = 64
TOKENS = 4096
SLOTS = 16384
N_DP = 4


def draw_routes(key, part):
    base_key, bias_key, hot_key, parity_key = jax.random.split(jax.random.fold_in(key, 17), 4)
    base_score = jax.random.randint(base_key, (TOKENS, EXPERTS), 0, 1 << 20)
    bias_score = jax.random.randint(bias_key, (EXPERTS,), 0, 3) * (1 << 19)
    windows = EXPERTS // EXP_DEV
    hot_expert = jax.random.randint(hot_key, (), 0, windows) * EXP_DEV
    parity = jax.random.randint(parity_key, (), 0, 2)
    row_ids = jnp.arange(TOKENS, dtype=jnp.int32)
    column_ids = jnp.arange(EXPERTS, dtype=jnp.int32)
    lifted = ((row_ids + parity) % 2 == 0)[:, None] & (column_ids == hot_expert)[None, :]
    scores = base_score + bias_score[None, :] + jnp.where(lifted, 1 << 21, 0)
    scores = scores * EXPERTS + column_ids[None, :]
    picked = lax.top_k(scores, TOP)[1]
    return picked.astype(jnp.int32)


def block_levels(own_key, dims, cuts, smallest, largest):
    loudness = 1.0
    for dim, parts in cuts:
        heights = jax.random.uniform(jax.random.fold_in(jax.random.fold_in(own_key, 6), dim), (parts,), jnp.float32, smallest / len(cuts), largest / len(cuts))
        loudness = loudness * jnp.repeat(jnp.exp(heights), dims[dim] // parts).reshape((-1,) + (1,) * (len(dims) - 1 - dim))
    return loudness


def noise(own_key, shape, spread, most, cuts=(), kind=jnp.bfloat16):
    array = spread * jax.random.normal(own_key, shape, jnp.float32)
    if cuts:
        array = array * block_levels(own_key, shape, cuts, -0.22, 0.18)
    return jnp.clip(array, -most, most).astype(kind)


def setup_inputs(seed: int = 0) -> dict:
    streams_of = jax.random.split(jax.random.key(seed), 8)
    tokens = noise(streams_of[0], (TOKENS, D), 1.0, 6.0, ((0, 32),))
    out_grad = noise(streams_of[1], (TOKENS, D), 0.05, 0.29882812, ((0, 32),))
    probs = jnp.clip(0.049804688 + 0.4501953 * jax.random.uniform(streams_of[2], (TOKENS, TOP), jnp.float32) ** block_levels(streams_of[2], (TOKENS, TOP), ((0, 32),), -0.2, 0.2), 0.049804688, 0.5).astype(jnp.bfloat16)
    routes = draw_routes(jax.random.fold_in(streams_of[7], 71), 0)
    saved_gate = noise(streams_of[4], (SLOTS, FF), 1.0, 6.0, ((0, 32),))
    saved_up = noise(streams_of[5], (SLOTS, FF), 1.0, 6.0, ((0, 32),))
    down_weight = noise(streams_of[6], (WINDOW, FF, D), FF ** -0.5, 0.21875, ((0, 8),))
    return {"tokens": tokens, "out_grad": out_grad, "probs": probs, "routes": routes, "saved_gate": saved_gate, "saved_up": saved_up, "down_weight": down_weight}


def reference(tokens, out_grad, probs, routes, saved_gate, saved_up, down_weight):
    owners = EXPERTS // EXP_DEV
    slot_rows = owners * CAP
    blocks = TOKENS // TOK_DEV
    in_window = (routes % EXP_DEV) == 0
    target = (routes // EXP_DEV).astype(jnp.int32)
    owner_ids = jnp.arange(owners, dtype=jnp.int32)
    routed = jnp.sum(((target[:, :, None] == owner_ids[None, None, :]) & in_window[:, :, None]).astype(jnp.int32), axis=1)
    routed = routed.reshape(blocks, TOK_DEV, owners)
    before = (jnp.cumsum(routed, axis=1) - routed).reshape(TOKENS, owners)
    position = jnp.take_along_axis(before, target, axis=1)
    retained = in_window & (position < CAP)
    token_ids = jnp.arange(TOKENS, dtype=jnp.int32)
    group_of = token_ids // (TOK_DEV * owners)
    source = (token_ids // TOK_DEV) % owners
    slot_total = N_DP * owners * slot_rows
    slot_index = ((group_of[:, None] * owners + target) * owners + source[:, None]) * CAP + position
    slot_index = jnp.where(retained, slot_index, slot_total).astype(jnp.int32)
    flat_index = slot_index.reshape(-1)
    holders = jnp.full((slot_total,), -1, jnp.int32).at[flat_index].set(
        jnp.broadcast_to(token_ids[:, None], slot_index.shape).reshape(-1), mode="drop")
    weight_of = jnp.zeros((slot_total,), jnp.float32).at[flat_index].set(
        probs.astype(jnp.float32).reshape(-1), mode="drop")
    holders = holders.reshape(N_DP, owners, slot_rows).transpose(1, 0, 2)
    weight_of = weight_of.reshape(N_DP, owners, slot_rows).transpose(1, 0, 2)
    gates = saved_gate.reshape(N_DP, owners, slot_rows, FF).transpose(1, 0, 2, 3)
    ups = saved_up.reshape(N_DP, owners, slot_rows, FF).transpose(1, 0, 2, 3)

    def one_expert(pieces):
        held, weight, gate_pre, up_pre, matrix = pieces
        filled = held >= 0
        safe_rows = jnp.maximum(held, 0)
        rows_x = jnp.where(filled[..., None], tokens[safe_rows], jnp.zeros((), tokens.dtype))
        rows_dy = jnp.where(filled[..., None], out_grad[safe_rows], jnp.zeros((), out_grad.dtype))
        gate_act = jax.nn.silu(gate_pre.astype(jnp.float32))
        hidden = (gate_act * up_pre.astype(jnp.float32)).astype(jnp.bfloat16)
        back_grad = jnp.einsum("grd,fd->grf", rows_dy.astype(jnp.float32), matrix.astype(jnp.float32))
        slot_grad = jnp.sum(hidden.astype(jnp.float32) * back_grad, axis=-1)
        scaled = (weight[..., None] * rows_dy.astype(jnp.float32)).astype(jnp.bfloat16)
        grad_pre = (weight[..., None] * back_grad * gate_act).astype(jnp.bfloat16)
        down_grad = jnp.einsum("grf,grd->fd", hidden.astype(jnp.float32), scaled.astype(jnp.float32))
        up_terms = jnp.einsum("grd,grf->gdf", rows_x.astype(jnp.float32), grad_pre.astype(jnp.float32))
        up_terms = lax.optimization_barrier(up_terms.astype(jnp.bfloat16)).astype(jnp.float32)
        up_grad = jnp.sum(up_terms, axis=0).astype(jnp.bfloat16)
        return down_grad, up_grad, slot_grad

    grad_down, grad_up, slot_grad = lax.map(one_expert, (holders, weight_of, gates, ups, down_weight))
    slot_flat = slot_grad.transpose(1, 0, 2).reshape(-1)
    prob_grad = jnp.where(retained, slot_flat[jnp.minimum(slot_index, slot_total - 1)], jnp.zeros((), jnp.float32))
    return grad_down, grad_up, prob_grad.astype(jnp.float32)
```

```python
import functools

import jax
import jax.numpy as jnp
from jax import lax
from jax.experimental import pallas as pl
from jax.experimental.pallas import tpu as pltpu
from jax.sharding import PartitionSpec as P

EXP_DEV = 4
X_PARTS = 2
X_CHUNKS = 2
COLUMNS = 512
VMEM = 48 * 1024 * 1024


COST = 0.0


def cost(flops, size):
    return pl.CostEstimate(
        flops=int(COST * flops), bytes_accessed=int(COST * size), transcendentals=0
    )


def after(value, *deps):
    return lax.optimization_barrier((value, *deps))[0]


def swap(value, axis, bit):
    size = lax.axis_size(axis)
    return lax.ppermute(value, axis, [(i, i ^ bit) for i in range(size)])


def exchange(table, axis):
    count = table.shape[0]
    bit = 1
    while bit < count:
        split = table.reshape(count // (2 * bit), 2, bit, table.shape[1])
        moved = swap(split[:, 1], axis, bit)
        table = jnp.stack([split[:, 0], moved], axis=1).reshape(table.shape)
        bit *= 2
    return table


def scatter_sum(kept, sent, axis):
    bit = 1
    while True:
        got = swap(sent, axis, bit)
        blocks = [kept[i] + got[i].astype(jnp.float32) for i in range(len(kept))]
        if len(blocks) == 1:
            return blocks[0]
        kept = blocks[0::2]
        sent = jnp.stack(blocks[1::2]).astype(jnp.bfloat16)
        bit *= 2


def slot_positions(table, capacity):
    tokens = table.shape[1]
    routed = table > 0
    earlier = (
        lax.broadcasted_iota(jnp.int32, (tokens, tokens), 0)
        < lax.broadcasted_iota(jnp.int32, (tokens, tokens), 1)
    )
    before = jnp.dot(
        jnp.where(routed, 1.0, 0.0).astype(jnp.bfloat16),
        jnp.where(earlier, 1.0, 0.0).astype(jnp.bfloat16),
        preferred_element_type=jnp.float32,
    ).astype(jnp.int32)
    return jnp.where(routed & (before < capacity), before, -1)


def place_kernel(parts, scaled, half, capacity, where, *refs):
    sources = 1 + max(source for part in parts for source, _, _ in part)
    tables, rows = refs[:sources], refs[sources : 2 * sources]
    outs = refs[2 * sources : 2 * sources + half]
    choices = refs[2 * sources + half :]
    step = pl.program_id(0)

    @pl.when(step == 0)
    def _():
        tokens = rows[0].shape[0]
        slot = lax.broadcasted_iota(jnp.int32, (capacity, tokens), 0)
        for s in range(sources):
            table = tables[s][...]
            position = slot_positions(table, capacity)
            value = table if scaled else jnp.where(table > 0, 1.0, 0.0)
            owner = lax.broadcasted_iota(jnp.int32, table.shape, 0)
            for k in range(half):
                mine = owner == (where[0] ^ k)
                wanted = jnp.sum(jnp.where(mine, position, 0), axis=0, keepdims=True)
                entry = jnp.sum(jnp.where(mine, value, 0.0), axis=0, keepdims=True)
                choices[s][k * capacity : (k + 1) * capacity, :] = jnp.where(
                    slot == wanted, entry, 0.0
                ).astype(jnp.bfloat16)

    for p, part in enumerate(parts):
        for source, start, end in part:

            @pl.when((step >= start) & (step < end))
            def _():
                placed = jnp.dot(
                    choices[source][...], rows[source][...], preferred_element_type=jnp.float32
                ).astype(jnp.bfloat16)
                for k in range(half):
                    outs[k][p * capacity : (p + 1) * capacity, :] = placed[
                        k * capacity : (k + 1) * capacity, :
                    ]


def place(where, tables, rows, maps, parts, steps, width, half, capacity, scaled):
    owners, tokens = tables[0].shape
    sources = len(tables)
    out_shape = (len(parts) * capacity, steps * width)
    return pl.pallas_call(
        functools.partial(place_kernel, parts, scaled, half, capacity),
        grid_spec=pltpu.PrefetchScalarGridSpec(
            num_scalar_prefetch=1,
            grid=(steps,),
            in_specs=[pl.BlockSpec((owners, tokens), lambda i, w: (0, 0))] * sources
            + [
                pl.BlockSpec((tokens, width), functools.partial(lambda m, i, w: (0, m(i, w)), m))
                for m in maps
            ],
            out_specs=[pl.BlockSpec((out_shape[0], width), lambda i, w: (0, i))] * half,
            scratch_shapes=[pltpu.VMEM((half * capacity, tokens), jnp.bfloat16)] * sources,
        ),
        out_shape=[jax.ShapeDtypeStruct(out_shape, jnp.bfloat16)] * half,
        compiler_params=pltpu.CompilerParams(vmem_limit_bytes=VMEM),
        cost_estimate=cost(
            2 * half * out_shape[0] * out_shape[1] * tokens,
            2 * (half * out_shape[0] + sources * tokens) * out_shape[1],
        ),
        name="place",
    )(where, *tables, *rows)


def down_kernel(pieces, first, weighted, matrix, *refs):
    dy = jnp.concatenate([ref[...] for ref in refs[:pieces]], axis=0)
    rest = refs[pieces:]
    back, kept, sent = rest[-3:]

    @pl.when(pl.program_id(0) == 0)
    def _():
        back[...] = jnp.zeros_like(back) if first else rest[0][...]

    back[...] += lax.dot_general(
        dy, matrix[...], (((1,), (1,)), ((), ())), preferred_element_type=jnp.float32
    )
    middle = kept.shape[0]
    kept[...] = jnp.dot(weighted[:middle, :], dy, preferred_element_type=jnp.float32)
    sent[...] = jnp.dot(weighted[middle:, :], dy, preferred_element_type=jnp.float32).astype(
        jnp.bfloat16
    )


def down_step(weighted, matrix, pieces, starts, capacity, back, start, width):
    hidden_width, slots = weighted.shape
    steps = width // COLUMNS
    offset = start // COLUMNS
    first = back is None
    constant = lambda i: (0, 0)
    column = lambda i: (0, i)
    middle = hidden_width // 2
    return pl.pallas_call(
        functools.partial(down_kernel, len(pieces), first),
        grid=(steps,),
        in_specs=[
            pl.BlockSpec((hidden_width, slots), constant),
            pl.BlockSpec((hidden_width, COLUMNS), lambda i: (0, i + offset)),
        ]
        + [
            pl.BlockSpec((capacity, COLUMNS), functools.partial(lambda o, i: (0, i + o), o // COLUMNS))
            for o in starts
        ]
        + ([] if first else [pl.BlockSpec((slots, hidden_width), constant)]),
        out_specs=[
            pl.BlockSpec((slots, hidden_width), constant),
            pl.BlockSpec((middle, COLUMNS), column),
            pl.BlockSpec((middle, COLUMNS), column),
        ],
        out_shape=[
            jax.ShapeDtypeStruct((slots, hidden_width), jnp.float32),
            jax.ShapeDtypeStruct((middle, width), jnp.float32),
            jax.ShapeDtypeStruct((middle, width), jnp.bfloat16),
        ],
        compiler_params=pltpu.CompilerParams(vmem_limit_bytes=VMEM),
        cost_estimate=cost(4 * slots * hidden_width * width, 2 * width * (slots + hidden_width) + 3 * width * hidden_width),
        name="down_step",
    )(weighted, matrix, *pieces, *([] if first else [back]))


def up_kernel(half, capacity, grad_pre, *refs):
    pieces = refs[:half]
    kept, sent = refs[half:]
    x = jnp.concatenate(
        [ref[:capacity, :] for ref in pieces] + [ref[capacity:, :] for ref in pieces], axis=0
    )
    width = kept.shape[0]
    contract = (((0,), (0,)), ((), ()))
    kept[...] = lax.dot_general(
        x[:, :width], grad_pre[...], contract, preferred_element_type=jnp.float32
    )
    sent[...] = lax.dot_general(
        x[:, width:], grad_pre[...], contract, preferred_element_type=jnp.float32
    ).astype(jnp.bfloat16)


def up_step(grad_pre, pieces, groups, capacity):
    slots, hidden_width = grad_pre.shape
    columns = pieces[0].shape[1]
    width = columns // groups
    pairs = groups // 2
    rows = pairs * width
    out = pl.BlockSpec((width, hidden_width), lambda i: (i, 0))
    return pl.pallas_call(
        functools.partial(up_kernel, len(pieces), capacity),
        grid=(pairs,),
        in_specs=[pl.BlockSpec((slots, hidden_width), lambda i: (0, 0))]
        + [pl.BlockSpec((piece.shape[0], 2 * width), lambda i: (0, i)) for piece in pieces],
        out_specs=[out, out],
        out_shape=[
            jax.ShapeDtypeStruct((rows, hidden_width), jnp.float32),
            jax.ShapeDtypeStruct((rows, hidden_width), jnp.bfloat16),
        ],
        compiler_params=pltpu.CompilerParams(vmem_limit_bytes=VMEM),
        cost_estimate=cost(2 * slots * hidden_width * columns, 2 * columns * slots + 3 * columns * hidden_width),
        name="up_step",
    )(grad_pre, *pieces)


def pick(table, index):
    return lax.dynamic_index_in_dim(table, index, 0, keepdims=False)


def per_device(tokens, out_grad, probs, routes, saved_gate, saved_up, down_weight):
    owners = lax.axis_size("expert")
    groups = lax.axis_size("dp")
    me = lax.axis_index("expert")
    group = lax.axis_index("dp")
    where = jnp.stack([me, group]).astype(jnp.int32)
    half = owners // 2
    tok_count, model_width = tokens.shape
    slot_rows, hidden_width = saved_gate.shape
    capacity = slot_rows // owners
    cuts = [0, model_width // 4, model_width]
    spans = list(zip(cuts[:-1], cuts[1:]))

    dy_far = []
    for lo, hi in spans:
        rows = out_grad[:, lo:hi]
        dy_far.append(swap(after(rows, dy_far[-1]) if dy_far else rows, "expert", half))

    owner_ids = jnp.arange(owners, dtype=jnp.int32) * EXP_DEV
    named = routes.T[None, :, :] == owner_ids[:, None, None]
    table_own = jnp.sum(jnp.where(named, probs.T[None, :, :].astype(jnp.float32), 0.0), axis=1)
    table_far = swap(table_own, "expert", half)

    order = me ^ jnp.arange(owners, dtype=jnp.int32)
    gate = saved_gate.reshape(owners, capacity, hidden_width)[order]
    up = saved_up.reshape(owners, capacity, hidden_width)[order]
    gate_act = jax.nn.silu(gate.reshape(slot_rows, hidden_width).astype(jnp.float32))
    hidden = (gate_act * up.reshape(slot_rows, hidden_width).astype(jnp.float32)).astype(
        jnp.bfloat16
    )
    block = hidden_width // groups
    hidden_t = hidden.T.reshape(groups, block, slot_rows)
    turns = list(range(0, groups, 2)) + list(range(1, groups, 2))
    hidden_t = jnp.concatenate([pick(hidden_t, group ^ r) for r in turns], axis=0)
    matrix = down_weight[0]

    def spread(sent):
        return [sent[0]] + [swap(sent[k], "expert", k) for k in range(1, half)]

    wide = model_width // COLUMNS
    extra = spans[0][1] // COLUMNS
    near = spread(
        place(
            where,
            [table_own, table_far],
            [out_grad, dy_far[0]],
            [lambda i, w: jnp.minimum(i, wide - 1), lambda i, w: jnp.maximum(i - wide, 0)],
            [[(0, 0, wide), (1, wide, wide + extra)]],
            wide + extra,
            COLUMNS,
            half,
            capacity,
            True,
        )
    )
    steps = (spans[1][1] - spans[1][0]) // COLUMNS
    far = spread(
        place(
            where,
            [table_far],
            [dy_far[1]],
            [lambda i, w: i],
            [[(0, 0, steps)]],
            steps,
            COLUMNS,
            half,
            capacity,
            True,
        )
    )

    share = model_width // groups
    part_width = share // X_PARTS
    width = part_width // X_CHUNKS
    x_far = []
    for part in range(X_PARTS):
        rows = jnp.concatenate(
            [
                tokens[:, b * share + part * part_width : b * share + (part + 1) * part_width]
                for b in range(groups)
            ],
            axis=1,
        )
        x_far.append(swap(after(rows, x_far[-1] if x_far else dy_far[-1]), "expert", half))

    down = []
    back = None
    for n, (lo, hi) in enumerate(spans):
        if n == 0:
            pieces, starts = near + near, [lo] * half + [model_width] * half
        else:
            pieces, starts = near + far, [lo] * half + [0] * half
            back = after(back, x_far[0])
        back, kept, sent = down_step(
            hidden_t, matrix, pieces, starts, capacity, back, lo, hi - lo
        )
        pairs = (groups // 2, block, hi - lo)
        down.append(scatter_sum(kept.reshape(pairs), sent.reshape(pairs), "dp"))
    down_share = jnp.concatenate(down, axis=1)

    slot_grad = jnp.sum(hidden.astype(jnp.float32) * back, axis=1)
    grad_pre = (back * gate_act).astype(jnp.bfloat16)
    returned = exchange(slot_grad.reshape(owners, capacity), "expert")[order]
    position_own = slot_positions(table_own, capacity)
    chosen_own = (
        lax.broadcasted_iota(jnp.int32, (owners, capacity, tok_count), 1) == position_own[:, None, :]
    )
    token_grad = jnp.sum(jnp.where(chosen_own, returned[:, :, None], 0.0), axis=1)
    token_grad = jnp.where(
        position_own >= 0, token_grad / jnp.where(table_own > 0, table_own, 1.0), 0.0
    )
    prob_grad = jnp.sum(jnp.where(named, token_grad[:, None, :], 0.0), axis=0).T

    up_parts = []
    for part in range(X_PARTS):
        for chunk in range(X_CHUNKS):
            n = len(up_parts)
            own_map = lambda i, w, c=n: (w[1] ^ i) * (X_PARTS * X_CHUNKS) + c
            far_map = lambda i, w, c=chunk: (w[1] ^ i) * X_CHUNKS + c
            far_rows = x_far[part]
            if n >= 2:
                far_rows = after(far_rows, down[n - 2])
            pieces = spread(
                place(
                    where,
                    [table_own, table_far],
                    [tokens, far_rows],
                    [own_map, far_map],
                    [[(0, 0, groups)], [(1, 0, groups)]],
                    groups,
                    width,
                    half,
                    capacity,
                    False,
                )
            )
            if n == 0:
                pieces[-1] = after(pieces[-1], x_far[1])
            kept, sent = up_step(grad_pre, pieces, groups, capacity)
            pairs = (groups // 2, width, hidden_width)
            up_parts.append(scatter_sum(kept.reshape(pairs), sent.reshape(pairs), "dp"))
    up_share = jnp.concatenate(up_parts, axis=0).astype(jnp.bfloat16)
    return down_share[None], up_share[None], prob_grad


def solution(mesh):
    in_specs = (
        P(("dp", "expert"), None),
        P(("dp", "expert"), None),
        P(("dp", "expert"), None),
        P(("dp", "expert"), None),
        P(("dp", "expert"), None),
        P(("dp", "expert"), None),
        P("expert", None, None),
    )
    out_specs = (P("expert", "dp", None), P("expert", "dp", None), P(("dp", "expert"), None))
    return jax.shard_map(
        per_device, mesh=mesh, in_specs=in_specs, out_specs=out_specs, check_vma=False
    )
```

```python
import functools

import jax
import jax.numpy as jnp
from jax import lax
from jax.experimental import pallas as pl
from jax.experimental.pallas import tpu as pltpu
from jax.sharding import PartitionSpec as P

EXP_DEV = 4
DY_PARTS = 2
X_PARTS = 2
X_CHUNKS = 4
VMEM = 32 * 1024 * 1024
COST = 0.0


def cost(flops, size):
    return pl.CostEstimate(
        flops=int(COST * flops), bytes_accessed=int(COST * size), transcendentals=0
    )


def after(value, *deps):
    return lax.optimization_barrier((value, *deps))[0]


def swap(value, axis, bit):
    size = lax.axis_size(axis)
    return lax.ppermute(value, axis, [(i, i ^ bit) for i in range(size)])


def exchange(table, axis, bits):
    count = table.shape[0]
    for bit in bits:
        split = table.reshape(count // (2 * bit), 2, bit, table.shape[1])
        moved = swap(split[:, 1], axis, bit)
        table = jnp.stack([split[:, 0], moved], axis=1).reshape(table.shape)
    return table


def chip_sum(kept, sent):
    bit = 2
    if isinstance(sent, list):
        split = sent[0].shape[-1]
        halves = [
            chip_sum([k[:, i * split : (i + 1) * split] for k in kept], piece)
            for i, piece in enumerate(sent)
        ]
        return jnp.concatenate(halves, axis=1)
    while True:
        got = swap(sent, "dp", bit)
        kept = [kept[i] + got[i].astype(jnp.float32) for i in range(len(kept))]
        if len(kept) == 1:
            return kept[0]
        kept, sent = kept[0::2], jnp.stack(kept[1::2]).astype(jnp.bfloat16)
        bit *= 2


def slot_positions(table, capacity):
    tokens = table.shape[1]
    routed = table > 0
    earlier = (
        lax.broadcasted_iota(jnp.int32, (tokens, tokens), 0)
        < lax.broadcasted_iota(jnp.int32, (tokens, tokens), 1)
    )
    before = jnp.dot(
        jnp.where(routed, 1.0, 0.0).astype(jnp.bfloat16),
        jnp.where(earlier, 1.0, 0.0).astype(jnp.bfloat16),
        preferred_element_type=jnp.float32,
    ).astype(jnp.int32)
    return jnp.where(routed & (before < capacity), before, -1)


def place_kernel(blocks, peers, scaled, capacity, where, tables, *refs):
    rows = refs[:blocks]
    outs = refs[blocks : blocks + len(peers)]
    choices = refs[-1]
    tokens = tables.shape[2]
    cores = tables.shape[0] // blocks

    @pl.when(pl.program_id(0) == 0)
    def _():
        slot = lax.broadcasted_iota(jnp.int32, (capacity, tokens), 0)
        for s in range(tables.shape[0]):
            table = tables[s]
            position = slot_positions(table, capacity)
            value = table if scaled else jnp.where(table > 0, 1.0, 0.0)
            owner = lax.broadcasted_iota(jnp.int32, table.shape, 0)
            for n, k in enumerate(peers):
                mine = owner == (where[0] ^ k)
                wanted = jnp.sum(jnp.where(mine, position, 0), axis=0, keepdims=True)
                entry = jnp.sum(jnp.where(mine, value, 0.0), axis=0, keepdims=True)
                choices[s, n * capacity : (n + 1) * capacity, :] = jnp.where(
                    slot == wanted, entry, 0.0
                ).astype(jnp.bfloat16)

    for s in range(tables.shape[0]):
        first = (s % cores) * tokens
        placed = jnp.dot(
            choices[s],
            rows[s // cores][first : first + tokens, :],
            preferred_element_type=jnp.float32,
        ).astype(jnp.bfloat16)
        for n in range(len(peers)):
            outs[n][s * capacity : (s + 1) * capacity, :] = placed[
                n * capacity : (n + 1) * capacity, :
            ]


def place(where, tables, rows, maps, steps, width, peers, capacity, scaled):
    sources, owners, tokens = tables.shape
    out_shape = (sources * capacity, steps * width)
    return pl.pallas_call(
        functools.partial(place_kernel, len(rows), peers, scaled, capacity),
        grid_spec=pltpu.PrefetchScalarGridSpec(
            num_scalar_prefetch=1,
            grid=(steps,),
            in_specs=[pl.BlockSpec((sources, owners, tokens), lambda i, w: (0, 0, 0))]
            + [
                pl.BlockSpec((r.shape[0], width), functools.partial(lambda m, i, w: (0, m(i)), m))
                for r, m in zip(rows, maps)
            ],
            out_specs=[pl.BlockSpec((out_shape[0], width), lambda i, w: (0, i))] * len(peers),
            scratch_shapes=[pltpu.VMEM((sources, len(peers) * capacity, tokens), jnp.bfloat16)],
        ),
        out_shape=[jax.ShapeDtypeStruct(out_shape, jnp.bfloat16)] * len(peers),
        compiler_params=pltpu.CompilerParams(vmem_limit_bytes=VMEM),
        cost_estimate=cost(
            2 * len(peers) * out_shape[0] * out_shape[1] * tokens,
            2 * (len(peers) + 1) * out_shape[0] * out_shape[1],
        ),
        name="place",
    )(where, tables, *rows)


def down_kernel(count, hidden_t, *refs):
    dy = jnp.concatenate([ref[...] for ref in refs[:count]], axis=0)
    kept, sent = refs[count], refs[count + 1 :]
    middle = kept.shape[0]
    kept[...] = jnp.dot(hidden_t[:middle, :], dy, preferred_element_type=jnp.float32)
    other = jnp.dot(hidden_t[middle:, :], dy, preferred_element_type=jnp.float32)
    for n, out in enumerate(sent):

        @pl.when(pl.program_id(0) * len(sent) // pl.num_programs(0) == n)
        def _():
            out[...] = other.astype(jnp.bfloat16)


def down_step(hidden_t, near, far, pairs, share, first):
    hidden_width, slots = hidden_t.shape
    total = far[0].shape[1]
    width = share // 2
    steps = total // width
    column = lambda i: (0, i)
    middle = hidden_width // 2
    kept, *sent = pl.pallas_call(
        functools.partial(down_kernel, len(near) + len(far)),
        grid=(steps,),
        in_specs=[pl.BlockSpec((hidden_width, slots), lambda i: (0, 0))]
        + [pl.BlockSpec((piece.shape[0], width), lambda i: (0, 2 * first + i)) for piece in near]
        + [pl.BlockSpec((piece.shape[0], width), column) for piece in far],
        out_specs=[
            pl.BlockSpec((middle, width), column),
            pl.BlockSpec((middle, width), lambda i: (0, jnp.minimum(i, steps // 2 - 1))),
            pl.BlockSpec((middle, width), lambda i: (0, jnp.maximum(i - steps // 2, 0))),
        ],
        out_shape=[jax.ShapeDtypeStruct((middle, total), jnp.float32)]
        + [jax.ShapeDtypeStruct((middle, total // 2), jnp.bfloat16)] * 2,
        compiler_params=pltpu.CompilerParams(vmem_limit_bytes=VMEM),
        cost_estimate=cost(
            2 * slots * hidden_width * total, 2 * total * slots + 3 * total * hidden_width
        ),
        name="down_step",
    )(hidden_t, *near, *far)
    kept = kept.reshape(pairs, middle // pairs, total)
    sent = [piece.reshape(pairs, middle // pairs, total // 2) for piece in sent]
    return [kept[i] for i in range(pairs)], sent


def back_kernel(count, where, matrix, *refs):
    back = refs[-1]

    @pl.when(pl.program_id(0) == 0)
    def _():
        back[...] = jnp.zeros_like(back) if len(refs) == count + 1 else refs[count][...]

    dy = jnp.concatenate([ref[...] for ref in refs[:count]], axis=0)
    back[...] += lax.dot_general(
        dy, matrix[...], (((1,), (1,)), ((), ())), preferred_element_type=jnp.float32
    )


def back_step(where, matrix, near, far, share, first, back):
    hidden_width = matrix.shape[0]
    pieces = near + far
    total = far[0].shape[1]
    slots = sum(piece.shape[0] for piece in pieces)
    before = [] if back is None else [back]
    whole = pl.BlockSpec((slots, hidden_width), lambda i, w: (0, 0))
    return pl.pallas_call(
        functools.partial(back_kernel, len(pieces)),
        grid_spec=pltpu.PrefetchScalarGridSpec(
            num_scalar_prefetch=1,
            grid=(total // share,),
            in_specs=[pl.BlockSpec((hidden_width, share), lambda i, w: (0, w[1] % 2 + 2 * (first + i)))]
            + [pl.BlockSpec((piece.shape[0], share), lambda i, w: (0, first + i)) for piece in near]
            + [pl.BlockSpec((piece.shape[0], share), lambda i, w: (0, i)) for piece in far]
            + [whole] * len(before),
            out_specs=whole,
        ),
        out_shape=jax.ShapeDtypeStruct((slots, hidden_width), jnp.float32),
        compiler_params=pltpu.CompilerParams(vmem_limit_bytes=VMEM),
        cost_estimate=cost(
            2 * slots * hidden_width * total, 2 * total * (slots + hidden_width)
        ),
        name="back_step",
    )(where, matrix, *pieces, *before)


def up_kernel(count, grad_pre, *refs):
    even, odd = refs[:count], refs[count : 2 * count]
    kept, sent = refs[2 * count :]
    contract = (((0,), (0,)), ((), ()))
    for pieces, out in ((even, kept), (odd, sent)):
        x = jnp.concatenate([ref[...] for ref in pieces], axis=0)
        out[...] = lax.dot_general(
            x, grad_pre[...], contract, preferred_element_type=jnp.float32
        ).astype(out.dtype)


def up_step(grad_pre, pieces, chunk, per, chips):
    slots, hidden_width = grad_pre.shape
    width = pieces[0].shape[1] // (per * chips)
    rows = pieces[0].shape[0] // 2
    pairs = chips // 2
    pieces = pieces + pieces

    def specs(odd):
        out = []
        for n in range(len(pieces)):
            far = 2 * n // len(pieces)
            index = lambda i, far=far: (far, (2 * i + odd) * per + chunk)
            out.append(pl.BlockSpec((rows, width), index))
        return out

    kept, sent = pl.pallas_call(
        functools.partial(up_kernel, len(pieces)),
        grid=(pairs,),
        in_specs=[pl.BlockSpec((slots, hidden_width), lambda i: (0, 0))] + specs(0) + specs(1),
        out_specs=[pl.BlockSpec((width, hidden_width), lambda i: (i, 0))] * 2,
        out_shape=[
            jax.ShapeDtypeStruct((pairs * width, hidden_width), jnp.float32),
            jax.ShapeDtypeStruct((pairs * width, hidden_width), jnp.bfloat16),
        ],
        compiler_params=pltpu.CompilerParams(vmem_limit_bytes=VMEM),
        cost_estimate=cost(
            2 * slots * hidden_width * chips * width,
            2 * chips * width * slots + 3 * chips * width * hidden_width,
        ),
        name="up_step",
    )(grad_pre, *pieces, *pieces)
    kept = kept.reshape(pairs, width, hidden_width)
    return [kept[i] for i in range(pairs)], sent.reshape(pairs, width, hidden_width)


def pick(table, index):
    return lax.dynamic_index_in_dim(table, index, 0, keepdims=False)


def per_device(tokens, out_grad, probs, routes, saved_gate, saved_up, down_weight):
    owners = lax.axis_size("expert")
    groups = lax.axis_size("dp")
    me = lax.axis_index("expert")
    group = lax.axis_index("dp")
    where = jnp.stack([me, group]).astype(jnp.int32)
    half = owners // 2
    chips = groups // 2
    tok_count, model_width = tokens.shape
    slot_rows, hidden_width = saved_gate.shape
    capacity = slot_rows // owners
    share = model_width // groups
    peers = list(range(0, half, 2))

    core = group % 2
    def columns(rows, block, lo, hi):
        return lax.dynamic_slice_in_dim(rows, block * share + lo, hi - lo, 1)

    def both_cores(rows, blocks, lo, hi):
        mine = jnp.concatenate([columns(rows, b, lo, hi) for b in blocks], axis=1)
        other = jnp.concatenate([columns(rows, b ^ 1, lo, hi) for b in blocks], axis=1)
        return jnp.concatenate([mine, swap(other, "dp", 1)], axis=0)

    blocks = [2 * r + core for r in range(chips)]
    per_part = chips // DY_PARTS
    dy_own = both_cores(out_grad, [2 * r + core for r in range(chips)], 0, share)
    dy_parts = [
        dy_own[:, h * per_part * share : (h + 1) * per_part * share] for h in range(DY_PARTS)
    ]

    owner_ids = jnp.arange(owners, dtype=jnp.int32) * EXP_DEV
    named = routes.T[None, :, :] == owner_ids[:, None, None]
    table_own = jnp.sum(jnp.where(named, probs.T[None, :, :].astype(jnp.float32), 0.0), axis=1)
    tables_core = jnp.stack([table_own, swap(table_own, "dp", 1)])
    tables_next = swap(after(tables_core, dy_parts[0]), "expert", 1)
    tables_near = jnp.concatenate([tables_core, tables_next])
    tables_far = swap(tables_near, "expert", half)

    peers = list(range(0, half, 2))
    same = lambda i: i

    def spread(sent):
        return [sent[0]] + [swap(sent[n], "expert", peers[n]) for n in range(1, len(peers))]

    def place_rows(tables, rows, scaled, steps=None, width=None, index=same):
        width = width or share
        steps = steps or rows[0].shape[1] // width
        maps = [index] * len(rows)
        return place(where, tables, rows, maps, steps, width, peers, capacity, scaled)

    dy_next = swap(after(dy_own, tables_next), "expert", 1)
    dy_far0 = swap(dy_parts[0], "expert", half)
    dy_from_own = place_rows(tables_core, [after(dy_own, tables_next)], True)
    placed = dy_from_own[0]
    dy_from_own = spread(dy_from_own)
    dy_next, dy_far0, dy_from_own, tables_far, dy1 = lax.optimization_barrier(
        (dy_next, dy_far0, dy_from_own, tables_far, dy_parts[1])
    )

    dy_far1 = swap(dy1, "expert", half)
    dy_from_next = spread(place_rows(tables_next, [dy_next], True))
    dy_far_next0 = swap(dy_far0, "expert", 1)
    x_own = both_cores(tokens, [group ^ (2 * r) for r in range(chips)], 0, share)
    part_width = share // X_PARTS
    x_parts = [
        jnp.concatenate(
            [
                x_own[:, r * share + p * part_width : r * share + (p + 1) * part_width]
                for r in range(chips)
            ],
            axis=1,
        )
        for p in range(X_PARTS)
    ]
    order = me ^ jnp.arange(owners, dtype=jnp.int32)
    saved = jnp.stack([saved_gate, saved_up]).reshape(2, owners, capacity, hidden_width)[:, order]
    dy_far1, dy_from_next, dy_far_next0, x_parts, saved = lax.optimization_barrier(
        (dy_far1, dy_from_next, dy_far_next0, x_parts, saved)
    )
    dy_near = [piece for pair in zip(dy_from_own, dy_from_next) for piece in pair]

    x_far0 = swap(x_parts[0], "expert", half)
    dy_spread0 = spread(place_rows(tables_far, [dy_far0, dy_far_next0], True))
    dy_far_next1 = swap(dy_far1, "expert", 1)
    x_next0 = swap(x_parts[0], "expert", 1)
    saved = jnp.stack([after(saved, dy_far_next1), swap(saved, "dp", 1)], axis=2)
    saved = saved.reshape(2, 2 * slot_rows, hidden_width).astype(jnp.float32)
    gate_act = jax.nn.silu(saved[0])
    hidden = (gate_act * saved[1]).astype(jnp.bfloat16)
    block = hidden_width // groups
    hidden_t = hidden.T.reshape(groups, block, 2 * slot_rows)
    rows_order = [m for m in range(groups) if not m & 2] + [m for m in range(groups) if m & 2]
    hidden_t = jnp.concatenate([pick(hidden_t, group ^ m) for m in rows_order], axis=0)
    matrix = down_weight[0]
    x_far0, dy_spread0, dy_far_next1, x_next0, x_parts, hidden_t = lax.optimization_barrier(
        (x_far0, dy_spread0, dy_far_next1, x_next0, x_parts, hidden_t)
    )

    x_far1 = swap(x_parts[1], "expert", half)
    dy_spread1 = spread(place_rows(tables_far, [dy_far1, dy_far_next1], True))
    x_far_next0 = swap(x_far0, "expert", 1)
    x_next1 = swap(x_parts[1], "expert", 1)
    held = after(dy_near[0], dy_spread1[0])
    terms = down_step(hidden_t, [held] + dy_near[1:], dy_spread0, chips // 2, share, 0)
    terms_kept = terms[0][0]
    down = [chip_sum(*terms)]
    x_far1, dy_spread1, x_far_next0, x_next1, terms_kept = lax.optimization_barrier(
        (x_far1, dy_spread1, x_far_next0, x_next1, terms_kept)
    )

    width = share // X_CHUNKS
    per = X_CHUNKS // X_PARTS
    tables_all = jnp.concatenate([tables_near, tables_far])
    x_far_next1 = swap(x_far1, "expert", 1)
    rows = [x_parts[0], x_next0, x_far0, x_far_next0]
    x_spread0 = place_rows(tables_all, rows, False, chips, part_width)
    near = [after(dy_near[0], x_spread0[0], x_far_next1)] + dy_near[1:]
    x_spread0 = spread(x_spread0)
    terms = down_step(hidden_t, near, dy_spread1, chips // 2, share, per_part)
    near[0] = after(near[0], terms[0][0])
    down.append(chip_sum(*terms))
    back = back_step(where, matrix, near, dy_spread0, share, 0, None)
    back = back_step(where, matrix, near, dy_spread1, share, per_part, back)
    back = back.reshape(owners, 2, capacity, hidden_width)
    other = [swap(back[:, 1 - g].astype(jnp.bfloat16), "dp", 1) for g in range(2)]
    x_rows = [x_parts[1], x_next1, x_far1]
    x_far_next1, x_spread0 = lax.optimization_barrier((x_far_next1, x_spread0))
    x_spread1 = place_rows(
        tables_all, x_rows + [x_far_next1], False, chips, part_width
    )
    other[0] = after(other[0], x_spread1[0])
    back = jnp.stack([back[:, g] + other[g].astype(jnp.float32) for g in range(2)], axis=1)
    back = back.reshape(2 * slot_rows, hidden_width)
    grad_pre = (back * gate_act).astype(jnp.bfloat16)
    slot_grad = jnp.sum(
        (hidden.astype(jnp.float32) * back).reshape(owners, 2, capacity, hidden_width)[:, 0], axis=2
    )

    up_terms = [up_step(grad_pre, x_spread0, n, per, chips) for n in range(per)]
    up_parts = [chip_sum(*terms) for terms in up_terms]
    grad_pre = after(grad_pre, up_terms[-1][1])
    bits = [1 << n for n in range(owners.bit_length() - 1)]
    near_bits = [bit for bit in bits if bit in (1, half)]
    far_bits = [bit for bit in bits if bit not in (1, half)]
    returned = exchange(after(slot_grad, up_terms[-1][1]), "expert", near_bits)
    x_spread1 = spread(x_spread1)
    for n in range(per):
        grad_pre = after(grad_pre, up_parts[n], returned)
        up_terms.append(up_step(grad_pre, x_spread1, n, per, chips))
        grad_pre = after(grad_pre, up_terms[-1][1])
    up_parts += [chip_sum(*terms) for terms in up_terms[per:]]
    down_blocks = []
    for h in range(DY_PARTS):
        mine, other = down[h][:block], swap(after(down[h][block:], up_parts[0]), "dp", 1)
        for r in range(per_part):
            span = slice(r * share, (r + 1) * share)
            for c in range(2):
                down_blocks.append(jnp.where(core == c, mine[:, span], other[:, span]))
    down_share = jnp.concatenate(down_blocks, axis=1)
    returned = exchange(after(returned, up_parts[per]), "expert", far_bits)[order]
    position_own = slot_positions(table_own, capacity)
    chosen_own = (
        lax.broadcasted_iota(jnp.int32, (owners, capacity, tok_count), 1) == position_own[:, None, :]
    )
    token_grad = jnp.sum(jnp.where(chosen_own, returned[:, :, None], 0.0), axis=1)
    token_grad = jnp.where(
        position_own >= 0, token_grad / jnp.where(table_own > 0, table_own, 1.0), 0.0
    )
    prob_grad = jnp.sum(jnp.where(named, token_grad[:, None, :], 0.0), axis=0).T
    up_share = jnp.concatenate(up_parts, axis=0).astype(jnp.bfloat16)

    return down_share[None], up_share[None], prob_grad


def solution(mesh):
    in_specs = (
        P(("dp", "expert"), None),
        P(("dp", "expert"), None),
        P(("dp", "expert"), None),
        P(("dp", "expert"), None),
        P(("dp", "expert"), None),
        P(("dp", "expert"), None),
        P("expert", None, None),
    )
    out_specs = (P("expert", "dp", None), P("expert", "dp", None), P(("dp", "expert"), None))
    return jax.shard_map(
        per_device, mesh=mesh, in_specs=in_specs, out_specs=out_specs, check_vma=False
    )
```

```python
import functools

import jax
import jax.numpy as jnp
from jax import lax
from jax.experimental import pallas as pl
from jax.experimental.pallas import tpu as pltpu
from jax.sharding import PartitionSpec as P

EXP_DEV = 4
DY_PARTS = 2
X_PARTS = 2
X_CHUNKS = 4
VMEM = 32 * 1024 * 1024
COST = 0.0


def cost(flops, size):
    return pl.CostEstimate(
        flops=int(COST * flops), bytes_accessed=int(COST * size), transcendentals=0
    )


def after(value, *deps):
    return lax.optimization_barrier((value, *deps))[0]


def swap(value, axis, bit):
    size = lax.axis_size(axis)
    return lax.ppermute(value, axis, [(i, i ^ bit) for i in range(size)])


def exchange(table, axis, bits):
    count = table.shape[0]
    for bit in bits:
        split = table.reshape(count // (2 * bit), 2, bit, table.shape[1])
        moved = swap(split[:, 1], axis, bit)
        table = jnp.stack([split[:, 0], moved], axis=1).reshape(table.shape)
    return table


def chip_sum(kept, sent):
    bit = 2
    while True:
        got = swap(sent, "dp", bit)
        kept = [kept[i] + got[i].astype(jnp.float32) for i in range(len(kept))]
        if len(kept) == 1:
            return kept[0]
        kept, sent = kept[0::2], jnp.stack(kept[1::2]).astype(jnp.bfloat16)
        bit *= 2


def slot_positions(table, capacity):
    tokens = table.shape[1]
    routed = table > 0
    earlier = (
        lax.broadcasted_iota(jnp.int32, (tokens, tokens), 0)
        < lax.broadcasted_iota(jnp.int32, (tokens, tokens), 1)
    )
    before = jnp.dot(
        jnp.where(routed, 1.0, 0.0).astype(jnp.bfloat16),
        jnp.where(earlier, 1.0, 0.0).astype(jnp.bfloat16),
        preferred_element_type=jnp.float32,
    ).astype(jnp.int32)
    return jnp.where(routed & (before < capacity), before, -1)


def place_kernel(blocks, peers, scaled, capacity, where, tables, *refs):
    rows = refs[:blocks]
    outs = refs[blocks : blocks + len(peers)]
    choices = refs[-1]
    tokens = tables.shape[2]
    cores = tables.shape[0] // blocks

    @pl.when(pl.program_id(0) == 0)
    def _():
        slot = lax.broadcasted_iota(jnp.int32, (capacity, tokens), 0)
        for s in range(tables.shape[0]):
            table = tables[s]
            position = slot_positions(table, capacity)
            value = table if scaled else jnp.where(table > 0, 1.0, 0.0)
            owner = lax.broadcasted_iota(jnp.int32, table.shape, 0)
            for n, k in enumerate(peers):
                mine = owner == (where[0] ^ k)
                wanted = jnp.sum(jnp.where(mine, position, 0), axis=0, keepdims=True)
                entry = jnp.sum(jnp.where(mine, value, 0.0), axis=0, keepdims=True)
                choices[s, n * capacity : (n + 1) * capacity, :] = jnp.where(
                    slot == wanted, entry, 0.0
                ).astype(jnp.bfloat16)

    for s in range(tables.shape[0]):
        first = (s % cores) * tokens
        placed = jnp.dot(
            choices[s],
            rows[s // cores][first : first + tokens, :],
            preferred_element_type=jnp.float32,
        ).astype(jnp.bfloat16)
        for n in range(len(peers)):
            outs[n][s * capacity : (s + 1) * capacity, :] = placed[
                n * capacity : (n + 1) * capacity, :
            ]


def place(where, tables, rows, maps, steps, width, peers, capacity, scaled):
    sources, owners, tokens = tables.shape
    out_shape = (sources * capacity, steps * width)
    return pl.pallas_call(
        functools.partial(place_kernel, len(rows), peers, scaled, capacity),
        grid_spec=pltpu.PrefetchScalarGridSpec(
            num_scalar_prefetch=1,
            grid=(steps,),
            in_specs=[pl.BlockSpec((sources, owners, tokens), lambda i, w: (0, 0, 0))]
            + [
                pl.BlockSpec((r.shape[0], width), functools.partial(lambda m, i, w: (0, m(i)), m))
                for r, m in zip(rows, maps)
            ],
            out_specs=[pl.BlockSpec((out_shape[0], width), lambda i, w: (0, i))] * len(peers),
            scratch_shapes=[pltpu.VMEM((sources, len(peers) * capacity, tokens), jnp.bfloat16)],
        ),
        out_shape=[jax.ShapeDtypeStruct(out_shape, jnp.bfloat16)] * len(peers),
        compiler_params=pltpu.CompilerParams(vmem_limit_bytes=VMEM),
        cost_estimate=cost(
            2 * len(peers) * out_shape[0] * out_shape[1] * tokens,
            2 * (len(peers) + 1) * out_shape[0] * out_shape[1],
        ),
        name="place",
    )(where, tables, *rows)


def down_kernel(count, hidden_t, *refs):
    dy = jnp.concatenate([ref[...] for ref in refs[:count]], axis=0)
    kept, sent = refs[count:]
    middle = kept.shape[0]
    kept[...] = jnp.dot(hidden_t[:middle, :], dy, preferred_element_type=jnp.float32)
    sent[...] = jnp.dot(hidden_t[middle:, :], dy, preferred_element_type=jnp.float32).astype(
        jnp.bfloat16
    )


def down_step(hidden_t, near, far, pairs, width, first):
    hidden_width, slots = hidden_t.shape
    total = far[0].shape[1]
    column = lambda i: (0, i)
    middle = hidden_width // 2
    kept, sent = pl.pallas_call(
        functools.partial(down_kernel, len(near) + len(far)),
        grid=(total // width,),
        in_specs=[pl.BlockSpec((hidden_width, slots), lambda i: (0, 0))]
        + [pl.BlockSpec((piece.shape[0], width), lambda i: (0, first + i)) for piece in near]
        + [pl.BlockSpec((piece.shape[0], width), column) for piece in far],
        out_specs=[pl.BlockSpec((middle, width), column)] * 2,
        out_shape=[
            jax.ShapeDtypeStruct((middle, total), jnp.float32),
            jax.ShapeDtypeStruct((middle, total), jnp.bfloat16),
        ],
        compiler_params=pltpu.CompilerParams(vmem_limit_bytes=VMEM),
        cost_estimate=cost(
            2 * slots * hidden_width * total, 2 * total * slots + 3 * total * hidden_width
        ),
        name="down_step",
    )(hidden_t, *near, *far)
    kept = kept.reshape(pairs, middle // pairs, total)
    return [kept[i] for i in range(pairs)], sent.reshape(pairs, middle // pairs, total)


def back_kernel(count, where, matrix, *refs):
    back = refs[-1]

    @pl.when(pl.program_id(0) == 0)
    def _():
        back[...] = jnp.zeros_like(back) if len(refs) == count + 1 else refs[count][...]

    dy = jnp.concatenate([ref[...] for ref in refs[:count]], axis=0)
    back[...] += lax.dot_general(
        dy, matrix[...], (((1,), (1,)), ((), ())), preferred_element_type=jnp.float32
    )


def back_step(where, matrix, near, far, share, first, back):
    hidden_width = matrix.shape[0]
    pieces = near + far
    total = far[0].shape[1]
    slots = sum(piece.shape[0] for piece in pieces)
    before = [] if back is None else [back]
    whole = pl.BlockSpec((slots, hidden_width), lambda i, w: (0, 0))
    return pl.pallas_call(
        functools.partial(back_kernel, len(pieces)),
        grid_spec=pltpu.PrefetchScalarGridSpec(
            num_scalar_prefetch=1,
            grid=(total // share,),
            in_specs=[pl.BlockSpec((hidden_width, share), lambda i, w: (0, w[1] % 2 + 2 * (first + i)))]
            + [pl.BlockSpec((piece.shape[0], share), lambda i, w: (0, first + i)) for piece in near]
            + [pl.BlockSpec((piece.shape[0], share), lambda i, w: (0, i)) for piece in far]
            + [whole] * len(before),
            out_specs=whole,
        ),
        out_shape=jax.ShapeDtypeStruct((slots, hidden_width), jnp.float32),
        compiler_params=pltpu.CompilerParams(vmem_limit_bytes=VMEM),
        cost_estimate=cost(
            2 * slots * hidden_width * total, 2 * total * (slots + hidden_width)
        ),
        name="back_step",
    )(where, matrix, *pieces, *before)


def up_kernel(count, grad_pre, *refs):
    even, odd = refs[:count], refs[count : 2 * count]
    kept, sent = refs[2 * count :]
    contract = (((0,), (0,)), ((), ()))
    for pieces, out in ((even, kept), (odd, sent)):
        x = jnp.concatenate([ref[...] for ref in pieces], axis=0)
        out[...] = lax.dot_general(
            x, grad_pre[...], contract, preferred_element_type=jnp.float32
        ).astype(out.dtype)


def up_step(grad_pre, pieces, chunk, per, chips):
    slots, hidden_width = grad_pre.shape
    width = pieces[0].shape[1] // (per * chips)
    rows = pieces[0].shape[0] // 2
    pairs = chips // 2
    pieces = pieces + pieces

    def specs(odd):
        out = []
        for n in range(len(pieces)):
            far = 2 * n // len(pieces)
            index = lambda i, far=far: (far, (2 * i + odd) * per + chunk)
            out.append(pl.BlockSpec((rows, width), index))
        return out

    kept, sent = pl.pallas_call(
        functools.partial(up_kernel, len(pieces)),
        grid=(pairs,),
        in_specs=[pl.BlockSpec((slots, hidden_width), lambda i: (0, 0))] + specs(0) + specs(1),
        out_specs=[pl.BlockSpec((width, hidden_width), lambda i: (i, 0))] * 2,
        out_shape=[
            jax.ShapeDtypeStruct((pairs * width, hidden_width), jnp.float32),
            jax.ShapeDtypeStruct((pairs * width, hidden_width), jnp.bfloat16),
        ],
        compiler_params=pltpu.CompilerParams(vmem_limit_bytes=VMEM),
        cost_estimate=cost(
            2 * slots * hidden_width * chips * width,
            2 * chips * width * slots + 3 * chips * width * hidden_width,
        ),
        name="up_step",
    )(grad_pre, *pieces, *pieces)
    kept = kept.reshape(pairs, width, hidden_width)
    return [kept[i] for i in range(pairs)], sent.reshape(pairs, width, hidden_width)


def pick(table, index):
    return lax.dynamic_index_in_dim(table, index, 0, keepdims=False)


def per_device(tokens, out_grad, probs, routes, saved_gate, saved_up, down_weight):
    owners = lax.axis_size("expert")
    groups = lax.axis_size("dp")
    me = lax.axis_index("expert")
    group = lax.axis_index("dp")
    where = jnp.stack([me, group]).astype(jnp.int32)
    half = owners // 2
    chips = groups // 2
    tok_count, model_width = tokens.shape
    slot_rows, hidden_width = saved_gate.shape
    capacity = slot_rows // owners
    share = model_width // groups
    peers = list(range(0, half, 2))

    core = group % 2
    def columns(rows, block, lo, hi):
        return lax.dynamic_slice_in_dim(rows, block * share + lo, hi - lo, 1)

    def both_cores(rows, blocks, lo, hi):
        mine = jnp.concatenate([columns(rows, b, lo, hi) for b in blocks], axis=1)
        other = jnp.concatenate([columns(rows, b ^ 1, lo, hi) for b in blocks], axis=1)
        return jnp.concatenate([mine, swap(other, "dp", 1)], axis=0)

    blocks = [2 * r + core for r in range(chips)]
    per_part = chips // DY_PARTS
    dy_own = both_cores(out_grad, [2 * r + core for r in range(chips)], 0, share)
    dy_parts = [
        dy_own[:, h * per_part * share : (h + 1) * per_part * share] for h in range(DY_PARTS)
    ]

    owner_ids = jnp.arange(owners, dtype=jnp.int32) * EXP_DEV
    named = routes.T[None, :, :] == owner_ids[:, None, None]
    table_own = jnp.sum(jnp.where(named, probs.T[None, :, :].astype(jnp.float32), 0.0), axis=1)
    tables_core = jnp.stack([table_own, swap(table_own, "dp", 1)])
    tables_next = swap(after(tables_core, dy_parts[0]), "expert", 1)
    tables_near = jnp.concatenate([tables_core, tables_next])
    tables_far = swap(tables_near, "expert", half)

    peers = list(range(0, half, 2))
    same = lambda i: i

    def spread(sent):
        return [sent[0]] + [swap(sent[n], "expert", peers[n]) for n in range(1, len(peers))]

    def place_rows(tables, rows, scaled, steps=None, width=None, index=same):
        width = width or share
        steps = steps or rows[0].shape[1] // width
        maps = [index] * len(rows)
        return place(where, tables, rows, maps, steps, width, peers, capacity, scaled)

    dy_next = swap(after(dy_own, tables_next), "expert", 1)
    dy_far0 = swap(dy_parts[0], "expert", half)
    dy_from_own = place_rows(tables_core, [after(dy_own, tables_next)], True)
    placed = dy_from_own[0]
    dy_from_own = spread(dy_from_own)
    dy_next, dy_far0, dy_from_own, tables_far, dy1 = lax.optimization_barrier(
        (dy_next, dy_far0, dy_from_own, tables_far, dy_parts[1])
    )

    dy_far1 = swap(dy1, "expert", half)
    dy_from_next = spread(place_rows(tables_next, [dy_next], True))
    dy_far_next0 = swap(dy_far0, "expert", 1)
    x_own = both_cores(after(tokens, placed), [group ^ (2 * r) for r in range(chips)], 0, share)
    part_width = share // X_PARTS
    x_parts = [
        jnp.concatenate(
            [
                x_own[:, r * share + p * part_width : r * share + (p + 1) * part_width]
                for r in range(chips)
            ],
            axis=1,
        )
        for p in range(X_PARTS)
    ]
    order = me ^ jnp.arange(owners, dtype=jnp.int32)
    saved = jnp.stack([after(saved_gate, placed), saved_up]).reshape(2, owners, capacity, hidden_width)[:, order]
    dy_far1, dy_from_next, dy_far_next0, x_parts, saved = lax.optimization_barrier(
        (dy_far1, dy_from_next, dy_far_next0, x_parts, saved)
    )
    dy_near = [piece for pair in zip(dy_from_own, dy_from_next) for piece in pair]

    x_far0 = swap(x_parts[0], "expert", half)
    dy_spread0 = spread(place_rows(tables_far, [dy_far0, dy_far_next0], True))
    dy_far_next1 = swap(dy_far1, "expert", 1)
    x_next0 = swap(x_parts[0], "expert", 1)
    saved = jnp.stack([after(saved, dy_far_next1), swap(saved, "dp", 1)], axis=2)
    saved = saved.reshape(2, 2 * slot_rows, hidden_width).astype(jnp.float32)
    gate_act = jax.nn.silu(saved[0])
    hidden = (gate_act * saved[1]).astype(jnp.bfloat16)
    block = hidden_width // groups
    hidden_t = hidden.T.reshape(groups, block, 2 * slot_rows)
    rows_order = [m for m in range(groups) if not m & 2] + [m for m in range(groups) if m & 2]
    hidden_t = jnp.concatenate([pick(hidden_t, group ^ m) for m in rows_order], axis=0)
    matrix = down_weight[0]
    x_far0, dy_spread0, dy_far_next1, x_next0, x_parts, hidden_t = lax.optimization_barrier(
        (x_far0, dy_spread0, dy_far_next1, x_next0, x_parts, hidden_t)
    )

    x_far1 = swap(x_parts[1], "expert", half)
    dy_spread1 = spread(place_rows(tables_far, [dy_far1, dy_far_next1], True))
    x_far_next0 = swap(x_far0, "expert", 1)
    x_next1 = swap(x_parts[1], "expert", 1)
    held = after(dy_near[0], dy_spread1[0])
    terms = down_step(hidden_t, [held] + dy_near[1:], dy_spread0, chips // 2, share, 0)
    terms_kept = terms[0][0]
    down = [chip_sum(*terms)]
    x_far1, dy_spread1, x_far_next0, x_next1, terms_kept = lax.optimization_barrier(
        (x_far1, dy_spread1, x_far_next0, x_next1, terms_kept)
    )

    width = share // X_CHUNKS
    per = X_CHUNKS // X_PARTS
    tables_all = jnp.concatenate([tables_near, tables_far])
    x_far_next1 = swap(x_far1, "expert", 1)
    rows = [x_parts[0], x_next0, x_far0, x_far_next0]
    x_spread0 = place_rows(tables_all, rows, False, chips, part_width)
    near = [after(dy_near[0], x_spread0[0], x_far_next1, down[0])] + dy_near[1:]
    x_spread0 = spread(x_spread0)
    terms = down_step(hidden_t, near, dy_spread1, chips // 2, share, per_part)
    near[0] = after(near[0], terms[0][0])
    down.append(chip_sum(*terms))
    back = back_step(where, matrix, near, dy_spread0, share, 0, None)
    back = back_step(where, matrix, near, dy_spread1, share, per_part, back)
    back = back.reshape(owners, 2, capacity, hidden_width)
    other = [swap(back[:, 1 - g].astype(jnp.bfloat16), "dp", 1) for g in range(2)]
    x_rows = [x_parts[1], x_next1, x_far1]
    x_far_next1, x_spread0 = lax.optimization_barrier((x_far_next1, x_spread0))
    x_spread1 = place_rows(
        tables_all, x_rows + [x_far_next1], False, chips, part_width
    )
    other[0] = after(other[0], x_spread1[0], down[1])
    back = jnp.stack([back[:, g] + other[g].astype(jnp.float32) for g in range(2)], axis=1)
    back = back.reshape(2 * slot_rows, hidden_width)
    grad_pre = (back * gate_act).astype(jnp.bfloat16)
    slot_grad = jnp.sum(
        (hidden.astype(jnp.float32) * back).reshape(owners, 2, capacity, hidden_width)[:, 0], axis=2
    )

    up_terms = [up_step(grad_pre, x_spread0, n, per, chips) for n in range(per)]
    up_parts = [chip_sum(*terms) for terms in up_terms]
    grad_pre = after(grad_pre, up_terms[-1][1])
    bits = [1 << n for n in range(owners.bit_length() - 1)]
    near_bits = [bit for bit in bits if bit in (1, half)]
    far_bits = [bit for bit in bits if bit not in (1, half)]
    returned = exchange(after(slot_grad, up_terms[-1][1]), "expert", near_bits)
    x_spread1 = spread(x_spread1)
    for n in range(per):
        grad_pre = after(grad_pre, up_parts[n], returned)
        up_terms.append(up_step(grad_pre, x_spread1, n, per, chips))
        grad_pre = after(grad_pre, up_terms[-1][1])
    up_parts += [chip_sum(*terms) for terms in up_terms[per:]]
    down_blocks = []
    for h in range(DY_PARTS):
        mine, other = down[h][:block], swap(after(down[h][block:], up_parts[0]), "dp", 1)
        for r in range(per_part):
            span = slice(r * share, (r + 1) * share)
            for c in range(2):
                down_blocks.append(jnp.where(core == c, mine[:, span], other[:, span]))
    down_share = jnp.concatenate(down_blocks, axis=1)
    returned = exchange(after(returned, up_parts[per]), "expert", far_bits)[order]
    position_own = slot_positions(table_own, capacity)
    chosen_own = (
        lax.broadcasted_iota(jnp.int32, (owners, capacity, tok_count), 1) == position_own[:, None, :]
    )
    token_grad = jnp.sum(jnp.where(chosen_own, returned[:, :, None], 0.0), axis=1)
    token_grad = jnp.where(
        position_own >= 0, token_grad / jnp.where(table_own > 0, table_own, 1.0), 0.0
    )
    prob_grad = jnp.sum(jnp.where(named, token_grad[:, None, :], 0.0), axis=0).T
    up_share = jnp.concatenate(up_parts, axis=0).astype(jnp.bfloat16)

    return down_share[None], up_share[None], prob_grad


def solution(mesh):
    in_specs = (
        P(("dp", "expert"), None),
        P(("dp", "expert"), None),
        P(("dp", "expert"), None),
        P(("dp", "expert"), None),
        P(("dp", "expert"), None),
        P(("dp", "expert"), None),
        P("expert", None, None),
    )
    out_specs = (P("expert", "dp", None), P("expert", "dp", None), P(("dp", "expert"), None))
    return jax.shard_map(
        per_device, mesh=mesh, in_specs=in_specs, out_specs=out_specs, check_vma=False
    )
```

```python
import functools

import jax
import jax.numpy as jnp
from jax import lax
from jax.experimental import pallas as pl
from jax.experimental.pallas import tpu as pltpu
from jax.sharding import PartitionSpec as P

EXP_DEV = 4
DY_PARTS = 2
X_PARTS = 2
X_CHUNKS = 4
VMEM = 32 * 1024 * 1024
COST = 0.0


def cost(flops, size):
    return pl.CostEstimate(
        flops=int(COST * flops), bytes_accessed=int(COST * size), transcendentals=0
    )


def after(value, *deps):
    return lax.optimization_barrier((value, *deps))[0]


def swap(value, axis, bit):
    size = lax.axis_size(axis)
    return lax.ppermute(value, axis, [(i, i ^ bit) for i in range(size)])


def exchange(table, axis, bits):
    count = table.shape[0]
    for bit in bits:
        split = table.reshape(count // (2 * bit), 2, bit, table.shape[1])
        moved = swap(split[:, 1], axis, bit)
        table = jnp.stack([split[:, 0], moved], axis=1).reshape(table.shape)
    return table


def chip_sum(kept, sent, raw=None):
    bit = 2
    while True:
        got = swap(sent, "dp", bit)
        if raw is not None:
            raw.append(got)
        kept = [kept[i] + got[i].astype(jnp.float32) for i in range(len(kept))]
        if len(kept) == 1:
            return kept[0]
        kept, sent = kept[0::2], jnp.stack(kept[1::2]).astype(jnp.bfloat16)
        bit *= 2


def slot_positions(table, capacity):
    tokens = table.shape[1]
    routed = table > 0
    earlier = (
        lax.broadcasted_iota(jnp.int32, (tokens, tokens), 0)
        < lax.broadcasted_iota(jnp.int32, (tokens, tokens), 1)
    )
    before = jnp.dot(
        jnp.where(routed, 1.0, 0.0).astype(jnp.bfloat16),
        jnp.where(earlier, 1.0, 0.0).astype(jnp.bfloat16),
        preferred_element_type=jnp.float32,
    ).astype(jnp.int32)
    return jnp.where(routed & (before < capacity), before, -1)


def choose_kernel(peers, capacity, where, tables, *outs):
    sources, owners, tokens = tables.shape
    slot = lax.broadcasted_iota(jnp.int32, (capacity, tokens), 0)
    owner = lax.broadcasted_iota(jnp.int32, (owners, tokens), 0)
    for s in range(sources):
        table = tables[s]
        position = slot_positions(table, capacity)
        for n, k in enumerate(peers):
            mine = owner == (where[0] ^ k)
            wanted = jnp.sum(jnp.where(mine, position, 0), axis=0, keepdims=True)
            entry = jnp.sum(jnp.where(mine, table, 0.0), axis=0, keepdims=True)
            for out, value in zip(outs, (entry, jnp.ones_like(entry))):
                out[s, n * capacity : (n + 1) * capacity, :] = jnp.where(
                    slot == wanted, value, 0.0
                ).astype(jnp.bfloat16)


def choose(where, tables, peers, capacity):
    sources, owners, tokens = tables.shape
    out = jax.ShapeDtypeStruct((sources, len(peers) * capacity, tokens), jnp.bfloat16)
    return pl.pallas_call(
        functools.partial(choose_kernel, peers, capacity),
        in_specs=[
            pl.BlockSpec(memory_space=pltpu.SMEM),
            pl.BlockSpec(memory_space=pltpu.VMEM),
        ],
        out_specs=[pl.BlockSpec(memory_space=pltpu.VMEM)] * 2,
        out_shape=[out] * 2,
        compiler_params=pltpu.CompilerParams(vmem_limit_bytes=VMEM),
        cost_estimate=cost(0, 0),
        name="choose",
    )(where, tables)


def place_kernel(blocks, peers, capacity, *refs):
    choices, rows, outs = refs[:blocks], refs[blocks : 2 * blocks], refs[2 * blocks :]
    cores, _, tokens = choices[0].shape
    for b in range(blocks):
        for c in range(cores):
            first = (b * cores + c) * capacity
            placed = jnp.dot(
                choices[b][c],
                rows[b][c * tokens : (c + 1) * tokens, :],
                preferred_element_type=jnp.float32,
            ).astype(jnp.bfloat16)
            for n in range(len(peers)):
                outs[n][first : first + capacity, :] = placed[n * capacity : (n + 1) * capacity, :]


def place(choices, rows, index, steps, width, peers, capacity):
    blocks = len(rows)
    cores = 2
    _, chosen, tokens = choices[0][0].shape
    out_shape = (blocks * cores * capacity, steps * width)
    return pl.pallas_call(
        functools.partial(place_kernel, blocks, peers, capacity),
        grid=(steps,),
        in_specs=[
            pl.BlockSpec((cores, chosen, tokens), functools.partial(lambda o, i: (o, 0, 0), o))
            for _, o in choices
        ]
        + [pl.BlockSpec((r.shape[0], width), lambda i: (0, index(i))) for r in rows],
        out_specs=[pl.BlockSpec((out_shape[0], width), lambda i: (0, i))] * len(peers),
        out_shape=[jax.ShapeDtypeStruct(out_shape, jnp.bfloat16)] * len(peers),
        compiler_params=pltpu.CompilerParams(vmem_limit_bytes=VMEM),
        cost_estimate=cost(
            2 * len(peers) * out_shape[0] * out_shape[1] * tokens,
            2 * (len(peers) + 1) * out_shape[0] * out_shape[1],
        ),
        name="place",
    )(*[array for array, _ in choices], *rows)


def down_kernel(count, hidden_t, *refs):
    dy = jnp.concatenate([ref[...] for ref in refs[:count]], axis=0)
    kept, sent = refs[count:]
    middle = kept.shape[0]
    kept[...] = jnp.dot(hidden_t[:middle, :], dy, preferred_element_type=jnp.float32)
    sent[...] = jnp.dot(hidden_t[middle:, :], dy, preferred_element_type=jnp.float32).astype(
        jnp.bfloat16
    )


def down_step(hidden_t, near, far, pairs, width, first):
    hidden_width, slots = hidden_t.shape
    total = far[0].shape[1]
    column = lambda i: (0, i)
    middle = hidden_width // 2
    kept, sent = pl.pallas_call(
        functools.partial(down_kernel, len(near) + len(far)),
        grid=(total // width,),
        in_specs=[pl.BlockSpec((hidden_width, slots), lambda i: (0, 0))]
        + [pl.BlockSpec((piece.shape[0], width), lambda i: (0, first + i)) for piece in near]
        + [pl.BlockSpec((piece.shape[0], width), column) for piece in far],
        out_specs=[pl.BlockSpec((middle, width), column)] * 2,
        out_shape=[
            jax.ShapeDtypeStruct((middle, total), jnp.float32),
            jax.ShapeDtypeStruct((middle, total), jnp.bfloat16),
        ],
        compiler_params=pltpu.CompilerParams(vmem_limit_bytes=VMEM),
        cost_estimate=cost(
            2 * slots * hidden_width * total, 2 * total * slots + 3 * total * hidden_width
        ),
        name="down_step",
    )(hidden_t, *near, *far)
    kept = kept.reshape(pairs, middle // pairs, total)
    return [kept[i] for i in range(pairs)], sent.reshape(pairs, middle // pairs, total)


def back_kernel(count, where, matrix, *refs):
    back = refs[-1]

    @pl.when(pl.program_id(0) == 0)
    def _():
        back[...] = jnp.zeros_like(back) if len(refs) == count + 1 else refs[count][...]

    dy = jnp.concatenate([ref[...] for ref in refs[:count]], axis=0)
    back[...] += lax.dot_general(
        dy, matrix[...], (((1,), (1,)), ((), ())), preferred_element_type=jnp.float32
    )


def back_step(where, matrix, near, far, share, first, back):
    hidden_width = matrix.shape[0]
    pieces = near + far
    total = far[0].shape[1]
    slots = sum(piece.shape[0] for piece in pieces)
    before = [] if back is None else [back]
    whole = pl.BlockSpec((slots, hidden_width), lambda i, w: (0, 0))
    return pl.pallas_call(
        functools.partial(back_kernel, len(pieces)),
        grid_spec=pltpu.PrefetchScalarGridSpec(
            num_scalar_prefetch=1,
            grid=(total // share,),
            in_specs=[pl.BlockSpec((hidden_width, share), lambda i, w: (0, w[1] % 2 + 2 * (first + i)))]
            + [pl.BlockSpec((piece.shape[0], share), lambda i, w: (0, first + i)) for piece in near]
            + [pl.BlockSpec((piece.shape[0], share), lambda i, w: (0, i)) for piece in far]
            + [whole] * len(before),
            out_specs=whole,
        ),
        out_shape=jax.ShapeDtypeStruct((slots, hidden_width), jnp.float32),
        compiler_params=pltpu.CompilerParams(vmem_limit_bytes=VMEM),
        cost_estimate=cost(
            2 * slots * hidden_width * total, 2 * total * (slots + hidden_width)
        ),
        name="back_step",
    )(where, matrix, *pieces, *before)


def up_kernel(count, grad_pre, *refs):
    even, odd = refs[:count], refs[count : 2 * count]
    kept, sent = refs[2 * count :]
    contract = (((0,), (0,)), ((), ()))
    for pieces, out in ((even, kept), (odd, sent)):
        x = jnp.concatenate([ref[...] for ref in pieces], axis=0)
        out[...] = lax.dot_general(
            x, grad_pre[...], contract, preferred_element_type=jnp.float32
        ).astype(out.dtype)


def up_step(grad_pre, pieces, chunk, per, chips):
    slots, hidden_width = grad_pre.shape
    width = pieces[0].shape[1] // (per * chips)
    rows = pieces[0].shape[0] // 2
    pairs = chips // 2
    pieces = pieces + pieces

    def specs(odd):
        out = []
        for n in range(len(pieces)):
            far = 2 * n // len(pieces)
            index = lambda i, far=far: (far, (2 * i + odd) * per + chunk)
            out.append(pl.BlockSpec((rows, width), index))
        return out

    kept, sent = pl.pallas_call(
        functools.partial(up_kernel, len(pieces)),
        grid=(pairs,),
        in_specs=[pl.BlockSpec((slots, hidden_width), lambda i: (0, 0))] + specs(0) + specs(1),
        out_specs=[pl.BlockSpec((width, hidden_width), lambda i: (i, 0))] * 2,
        out_shape=[
            jax.ShapeDtypeStruct((pairs * width, hidden_width), jnp.float32),
            jax.ShapeDtypeStruct((pairs * width, hidden_width), jnp.bfloat16),
        ],
        compiler_params=pltpu.CompilerParams(vmem_limit_bytes=VMEM),
        cost_estimate=cost(
            2 * slots * hidden_width * chips * width,
            2 * chips * width * slots + 3 * chips * width * hidden_width,
        ),
        name="up_step",
    )(grad_pre, *pieces, *pieces)
    kept = kept.reshape(pairs, width, hidden_width)
    return [kept[i] for i in range(pairs)], sent.reshape(pairs, width, hidden_width)


def pick(table, index):
    return lax.dynamic_index_in_dim(table, index, 0, keepdims=False)


def per_device(tokens, out_grad, probs, routes, saved_gate, saved_up, down_weight):
    owners = lax.axis_size("expert")
    groups = lax.axis_size("dp")
    me = lax.axis_index("expert")
    group = lax.axis_index("dp")
    where = jnp.stack([me, group]).astype(jnp.int32)
    half = owners // 2
    chips = groups // 2
    tok_count, model_width = tokens.shape
    slot_rows, hidden_width = saved_gate.shape
    capacity = slot_rows // owners
    share = model_width // groups
    peers = list(range(0, half, 2))

    core = group % 2
    def columns(rows, block, lo, hi):
        return lax.dynamic_slice_in_dim(rows, block * share + lo, hi - lo, 1)

    def both_cores(rows, blocks, lo, hi):
        mine = jnp.concatenate([columns(rows, b, lo, hi) for b in blocks], axis=1)
        other = jnp.concatenate([columns(rows, b ^ 1, lo, hi) for b in blocks], axis=1)
        return jnp.concatenate([mine, swap(other, "dp", 1)], axis=0)

    blocks = [2 * r + core for r in range(chips)]
    per_part = chips // DY_PARTS
    dy_own = both_cores(out_grad, [2 * r + core for r in range(chips)], 0, share)
    dy_parts = [
        dy_own[:, h * per_part * share : (h + 1) * per_part * share] for h in range(DY_PARTS)
    ]

    owner_ids = jnp.arange(owners, dtype=jnp.int32) * EXP_DEV
    named = routes.T[None, :, :] == owner_ids[:, None, None]
    table_own = jnp.sum(jnp.where(named, probs.T[None, :, :].astype(jnp.float32), 0.0), axis=1)
    tables_core = jnp.stack([table_own, swap(table_own, "dp", 1)])
    tables_next = swap(after(tables_core, dy_parts[0]), "expert", 1)
    tables_near = jnp.concatenate([tables_core, tables_next])
    tables_far = swap(tables_near, "expert", half)

    peers = list(range(0, half, 2))
    same = lambda i: i

    def spread(sent):
        return [sent[0]] + [swap(sent[n], "expert", peers[n]) for n in range(1, len(peers))]

    def place_rows(choices, rows, steps=None, width=None, index=same):
        width = width or share
        steps = steps or rows[0].shape[1] // width
        return place(choices, rows, index, steps, width, peers, capacity)

    scaled_near, plain_near = choose(where, tables_near, peers, capacity)

    dy_next = swap(after(dy_own, tables_next), "expert", 1)
    dy_far0 = swap(dy_parts[0], "expert", half)
    dy_from_own = place_rows([(scaled_near, 0)], [dy_own])
    placed = dy_from_own[0]
    dy_from_own = spread(dy_from_own)
    dy_next, dy_far0, dy_from_own, tables_far, dy1 = lax.optimization_barrier(
        (dy_next, dy_far0, dy_from_own, tables_far, dy_parts[1])
    )

    dy_far1 = swap(dy1, "expert", half)
    dy_from_next = spread(place_rows([(scaled_near, 1)], [dy_next]))
    dy_far_next0 = swap(dy_far0, "expert", 1)
    x_own = both_cores(after(tokens, placed), [group ^ (2 * r) for r in range(chips)], 0, share)
    part_width = share // X_PARTS
    x_parts = [
        jnp.concatenate(
            [
                x_own[:, r * share + p * part_width : r * share + (p + 1) * part_width]
                for r in range(chips)
            ],
            axis=1,
        )
        for p in range(X_PARTS)
    ]
    order = me ^ jnp.arange(owners, dtype=jnp.int32)
    saved = jnp.stack([after(saved_gate, placed), saved_up]).reshape(2, owners, capacity, hidden_width)[:, order]
    scaled_far, plain_far = choose(where, after(tables_far, dy_from_next[0]), peers, capacity)
    dy_far1, dy_from_next, dy_far_next0, x_parts, saved, scaled_far = lax.optimization_barrier(
        (dy_far1, dy_from_next, dy_far_next0, x_parts, saved, scaled_far)
    )
    dy_near = [piece for pair in zip(dy_from_own, dy_from_next) for piece in pair]

    x_far0 = swap(x_parts[0], "expert", half)
    dy_spread0 = spread(place_rows([(scaled_far, 0), (scaled_far, 1)], [dy_far0, dy_far_next0]))
    dy_far_next1 = swap(dy_far1, "expert", 1)
    x_next0 = swap(x_parts[0], "expert", 1)
    saved = jnp.stack([after(saved, dy_far_next1), swap(saved, "dp", 1)], axis=2)
    saved = saved.reshape(2, 2 * slot_rows, hidden_width).astype(jnp.float32)
    gate_act = jax.nn.silu(saved[0])
    hidden = (gate_act * saved[1]).astype(jnp.bfloat16)
    block = hidden_width // groups
    hidden_t = hidden.T.reshape(groups, block, 2 * slot_rows)
    rows_order = [m for m in range(groups) if not m & 2] + [m for m in range(groups) if m & 2]
    hidden_t = jnp.concatenate([pick(hidden_t, group ^ m) for m in rows_order], axis=0)
    matrix = down_weight[0]
    x_far0, dy_spread0, dy_far_next1, x_next0, x_parts, hidden_t = lax.optimization_barrier(
        (x_far0, dy_spread0, dy_far_next1, x_next0, x_parts, hidden_t)
    )

    x_far1 = swap(x_parts[1], "expert", half)
    dy_spread1 = spread(place_rows([(scaled_far, 0), (scaled_far, 1)], [dy_far1, dy_far_next1]))
    x_far_next0 = swap(x_far0, "expert", 1)
    x_next1 = swap(x_parts[1], "expert", 1)
    held = after(dy_near[0], dy_spread1[0])
    terms = down_step(hidden_t, [held] + dy_near[1:], dy_spread0, chips // 2, share, 0)
    terms_kept = terms[0][0]
    down = [chip_sum(*terms)]
    x_far1, dy_spread1, x_far_next0, x_next1, terms_kept = lax.optimization_barrier(
        (x_far1, dy_spread1, x_far_next0, x_next1, terms_kept)
    )

    width = share // X_CHUNKS
    per = X_CHUNKS // X_PARTS
    plain = [(plain_near, 0), (plain_near, 1), (plain_far, 0), (plain_far, 1)]
    x_far_next1 = swap(x_far1, "expert", 1)
    rows = [x_parts[0], x_next0, x_far0, x_far_next0]
    x_spread0 = place_rows(plain, rows, chips, part_width)
    near = [after(dy_near[0], x_spread0[0], x_far_next1, down[0])] + dy_near[1:]
    x_spread0 = spread(x_spread0)
    terms = down_step(hidden_t, near, dy_spread1, chips // 2, share, per_part)
    near[0] = after(near[0], terms[0][0])
    raw = []
    down.append(chip_sum(*terms, raw))
    back = back_step(where, matrix, near, dy_spread0, share, 0, None)
    back = back_step(where, matrix, near, dy_spread1, share, per_part, back)
    back = back.reshape(owners, 2, capacity, hidden_width)
    other = [swap(back[:, 1 - g].astype(jnp.bfloat16), "dp", 1) for g in range(2)]
    x_rows = [x_parts[1], x_next1, x_far1]
    x_far_next1, x_spread0 = lax.optimization_barrier((x_far_next1, x_spread0))
    x_spread1 = place_rows(
        plain, x_rows + [x_far_next1], chips, part_width
    )
    other[0] = after(other[0], x_spread1[0], raw[-1])
    back = jnp.stack([back[:, g] + other[g].astype(jnp.float32) for g in range(2)], axis=1)
    back = back.reshape(2 * slot_rows, hidden_width)
    grad_pre = (back * gate_act).astype(jnp.bfloat16)
    slot_grad = jnp.sum(
        (hidden.astype(jnp.float32) * back).reshape(owners, 2, capacity, hidden_width)[:, 0], axis=2
    )

    up_terms = [up_step(grad_pre, x_spread0, n, per, chips) for n in range(per)]
    up_parts = [chip_sum(*terms) for terms in up_terms]
    grad_pre = after(grad_pre, up_terms[-1][1])
    bits = [1 << n for n in range(owners.bit_length() - 1)]
    near_bits = [bit for bit in bits if bit in (1, half)]
    far_bits = [bit for bit in bits if bit not in (1, half)]
    returned = exchange(after(slot_grad, up_terms[-1][1]), "expert", near_bits)
    x_spread1 = spread(x_spread1)
    for n in range(per):
        grad_pre = after(grad_pre, up_parts[n])
        up_terms.append(up_step(grad_pre, x_spread1, n, per, chips))
        grad_pre = after(grad_pre, up_terms[-1][1])
    up_parts += [chip_sum(*terms) for terms in up_terms[per:]]
    down_blocks = []
    for h in range(DY_PARTS):
        mine, other = down[h][:block], swap(after(down[h][block:], up_parts[0]), "dp", 1)
        for r in range(per_part):
            span = slice(r * share, (r + 1) * share)
            for c in range(2):
                down_blocks.append(jnp.where(core == c, mine[:, span], other[:, span]))
    down_share = jnp.concatenate(down_blocks, axis=1)
    returned = exchange(after(returned, up_parts[per]), "expert", far_bits)[order]
    position_own = slot_positions(table_own, capacity)
    chosen_own = (
        lax.broadcasted_iota(jnp.int32, (owners, capacity, tok_count), 1) == position_own[:, None, :]
    )
    token_grad = jnp.sum(jnp.where(chosen_own, returned[:, :, None], 0.0), axis=1)
    token_grad = jnp.where(
        position_own >= 0, token_grad / jnp.where(table_own > 0, table_own, 1.0), 0.0
    )
    prob_grad = jnp.sum(jnp.where(named, token_grad[:, None, :], 0.0), axis=0).T
    up_share = jnp.concatenate(up_parts, axis=0).astype(jnp.bfloat16)

    return down_share[None], up_share[None], prob_grad


def solution(mesh):
    in_specs = (
        P(("dp", "expert"), None),
        P(("dp", "expert"), None),
        P(("dp", "expert"), None),
        P(("dp", "expert"), None),
        P(("dp", "expert"), None),
        P(("dp", "expert"), None),
        P("expert", None, None),
    )
    out_specs = (P("expert", "dp", None), P("expert", "dp", None), P(("dp", "expert"), None))
    return jax.shard_map(
        per_device, mesh=mesh, in_specs=in_specs, out_specs=out_specs, check_vma=False
    )
```

```python
import functools

import jax
import jax.numpy as jnp
from jax import lax
from jax.experimental import pallas as pl
from jax.experimental.pallas import tpu as pltpu
from jax.sharding import PartitionSpec as P

EXP_DEV = 4
DY_PARTS = 2
X_PARTS = 2
X_CHUNKS = 4
VMEM = 32 * 1024 * 1024
COST = 0.0


def cost(flops, size):
    return pl.CostEstimate(
        flops=int(COST * flops), bytes_accessed=int(COST * size), transcendentals=0
    )


def after(value, *deps):
    return lax.optimization_barrier((value, *deps))[0]


def swap(value, axis, bit):
    size = lax.axis_size(axis)
    return lax.ppermute(value, axis, [(i, i ^ bit) for i in range(size)])


def exchange(table, axis, bits):
    count = table.shape[0]
    for bit in bits:
        split = table.reshape(count // (2 * bit), 2, bit, table.shape[1])
        moved = swap(split[:, 1], axis, bit)
        table = jnp.stack([split[:, 0], moved], axis=1).reshape(table.shape)
    return table


def chip_sum(kept, sent, raw=None):
    bit = 2
    while True:
        got = swap(sent, "dp", bit)
        if raw is not None:
            raw.append(got)
        kept = [kept[i] + got[i].astype(jnp.float32) for i in range(len(kept))]
        if len(kept) == 1:
            return kept[0]
        kept, sent = kept[0::2], jnp.stack(kept[1::2]).astype(jnp.bfloat16)
        bit *= 2


def slot_positions(table, capacity):
    tokens = table.shape[1]
    routed = table > 0
    earlier = (
        lax.broadcasted_iota(jnp.int32, (tokens, tokens), 0)
        < lax.broadcasted_iota(jnp.int32, (tokens, tokens), 1)
    )
    before = jnp.dot(
        jnp.where(routed, 1.0, 0.0).astype(jnp.bfloat16),
        jnp.where(earlier, 1.0, 0.0).astype(jnp.bfloat16),
        preferred_element_type=jnp.float32,
    ).astype(jnp.int32)
    return jnp.where(routed & (before < capacity), before, -1)


def choose_kernel(peers, capacity, where, tables, *outs):
    sources, owners, tokens = tables.shape
    slot = lax.broadcasted_iota(jnp.int32, (capacity, tokens), 0)
    owner = lax.broadcasted_iota(jnp.int32, (owners, tokens), 0)
    for s in range(sources):
        table = tables[s]
        position = slot_positions(table, capacity)
        for n, k in enumerate(peers):
            mine = owner == (where[0] ^ k)
            wanted = jnp.sum(jnp.where(mine, position, 0), axis=0, keepdims=True)
            entry = jnp.sum(jnp.where(mine, table, 0.0), axis=0, keepdims=True)
            for out, value in zip(outs, (entry, jnp.ones_like(entry))):
                out[s, n * capacity : (n + 1) * capacity, :] = jnp.where(
                    slot == wanted, value, 0.0
                ).astype(jnp.bfloat16)


def choose(where, tables, peers, capacity):
    sources, owners, tokens = tables.shape
    out = jax.ShapeDtypeStruct((sources, len(peers) * capacity, tokens), jnp.bfloat16)
    return pl.pallas_call(
        functools.partial(choose_kernel, peers, capacity),
        in_specs=[
            pl.BlockSpec(memory_space=pltpu.SMEM),
            pl.BlockSpec(memory_space=pltpu.VMEM),
        ],
        out_specs=[pl.BlockSpec(memory_space=pltpu.VMEM)] * 2,
        out_shape=[out] * 2,
        compiler_params=pltpu.CompilerParams(vmem_limit_bytes=VMEM),
        cost_estimate=cost(0, 0),
        name="choose",
    )(where, tables)


def place_kernel(blocks, peers, capacity, *refs):
    choices, rows, outs = refs[:blocks], refs[blocks : 2 * blocks], refs[2 * blocks :]
    cores, _, tokens = choices[0].shape
    for b in range(blocks):
        for c in range(cores):
            first = (b * cores + c) * capacity
            placed = jnp.dot(
                choices[b][c],
                rows[b][c * tokens : (c + 1) * tokens, :],
                preferred_element_type=jnp.float32,
            ).astype(jnp.bfloat16)
            for n in range(len(peers)):
                outs[n][first : first + capacity, :] = placed[n * capacity : (n + 1) * capacity, :]


def place(choices, rows, index, steps, width, peers, capacity):
    blocks = len(rows)
    cores = 2
    _, chosen, tokens = choices[0][0].shape
    out_shape = (blocks * cores * capacity, steps * width)
    return pl.pallas_call(
        functools.partial(place_kernel, blocks, peers, capacity),
        grid=(steps,),
        in_specs=[
            pl.BlockSpec((cores, chosen, tokens), functools.partial(lambda o, i: (o, 0, 0), o))
            for _, o in choices
        ]
        + [pl.BlockSpec((r.shape[0], width), lambda i: (0, index(i))) for r in rows],
        out_specs=[pl.BlockSpec((out_shape[0], width), lambda i: (0, i))] * len(peers),
        out_shape=[jax.ShapeDtypeStruct(out_shape, jnp.bfloat16)] * len(peers),
        compiler_params=pltpu.CompilerParams(vmem_limit_bytes=VMEM),
        cost_estimate=cost(
            2 * len(peers) * out_shape[0] * out_shape[1] * tokens,
            2 * (len(peers) + 1) * out_shape[0] * out_shape[1],
        ),
        name="place",
    )(*[array for array, _ in choices], *rows)


def down_kernel(count, hidden_t, *refs):
    dy = jnp.concatenate([ref[...] for ref in refs[:count]], axis=0)
    kept, sent = refs[count:]
    middle = kept.shape[0]
    kept[...] = jnp.dot(hidden_t[:middle, :], dy, preferred_element_type=jnp.float32)
    sent[...] = jnp.dot(hidden_t[middle:, :], dy, preferred_element_type=jnp.float32).astype(
        jnp.bfloat16
    )


def down_step(hidden_t, near, far, pairs, width, first):
    hidden_width, slots = hidden_t.shape
    total = far[0].shape[1]
    column = lambda i: (0, i)
    middle = hidden_width // 2
    kept, sent = pl.pallas_call(
        functools.partial(down_kernel, len(near) + len(far)),
        grid=(total // width,),
        in_specs=[pl.BlockSpec((hidden_width, slots), lambda i: (0, 0))]
        + [pl.BlockSpec((piece.shape[0], width), lambda i: (0, first + i)) for piece in near]
        + [pl.BlockSpec((piece.shape[0], width), column) for piece in far],
        out_specs=[pl.BlockSpec((middle, width), column)] * 2,
        out_shape=[
            jax.ShapeDtypeStruct((middle, total), jnp.float32),
            jax.ShapeDtypeStruct((middle, total), jnp.bfloat16),
        ],
        compiler_params=pltpu.CompilerParams(vmem_limit_bytes=VMEM),
        cost_estimate=cost(
            2 * slots * hidden_width * total, 2 * total * slots + 3 * total * hidden_width
        ),
        name="down_step",
    )(hidden_t, *near, *far)
    kept = kept.reshape(pairs, middle // pairs, total)
    return [kept[i] for i in range(pairs)], sent.reshape(pairs, middle // pairs, total)


def back_kernel(count, where, matrix, *refs):
    back = refs[-1]

    @pl.when(pl.program_id(0) == 0)
    def _():
        back[...] = jnp.zeros_like(back) if len(refs) == count + 1 else refs[count][...]

    dy = jnp.concatenate([ref[...] for ref in refs[:count]], axis=0)
    back[...] += lax.dot_general(
        dy, matrix[...], (((1,), (1,)), ((), ())), preferred_element_type=jnp.float32
    )


def back_step(where, matrix, near, far, share, first, back):
    hidden_width = matrix.shape[0]
    pieces = near + far
    total = far[0].shape[1]
    slots = sum(piece.shape[0] for piece in pieces)
    before = [] if back is None else [back]
    whole = pl.BlockSpec((slots, hidden_width), lambda i, w: (0, 0))
    return pl.pallas_call(
        functools.partial(back_kernel, len(pieces)),
        grid_spec=pltpu.PrefetchScalarGridSpec(
            num_scalar_prefetch=1,
            grid=(total // share,),
            in_specs=[pl.BlockSpec((hidden_width, share), lambda i, w: (0, w[1] % 2 + 2 * (first + i)))]
            + [pl.BlockSpec((piece.shape[0], share), lambda i, w: (0, first + i)) for piece in near]
            + [pl.BlockSpec((piece.shape[0], share), lambda i, w: (0, i)) for piece in far]
            + [whole] * len(before),
            out_specs=whole,
        ),
        out_shape=jax.ShapeDtypeStruct((slots, hidden_width), jnp.float32),
        compiler_params=pltpu.CompilerParams(vmem_limit_bytes=VMEM),
        cost_estimate=cost(
            2 * slots * hidden_width * total, 2 * total * (slots + hidden_width)
        ),
        name="back_step",
    )(where, matrix, *pieces, *before)


def up_kernel(count, grad_pre, *refs):
    even, odd = refs[:count], refs[count : 2 * count]
    kept, sent = refs[2 * count :]
    contract = (((0,), (0,)), ((), ()))
    for pieces, out in ((even, kept), (odd, sent)):
        x = jnp.concatenate([ref[...] for ref in pieces], axis=0)
        out[...] = lax.dot_general(
            x, grad_pre[...], contract, preferred_element_type=jnp.float32
        ).astype(out.dtype)


def up_step(grad_pre, pieces, chunk, per, chips):
    slots, hidden_width = grad_pre.shape
    width = pieces[0].shape[1] // (per * chips)
    rows = pieces[0].shape[0] // 2
    pairs = chips // 2
    pieces = pieces + pieces

    def specs(odd):
        out = []
        for n in range(len(pieces)):
            far = 2 * n // len(pieces)
            index = lambda i, far=far: (far, (2 * i + odd) * per + chunk)
            out.append(pl.BlockSpec((rows, width), index))
        return out

    kept, sent = pl.pallas_call(
        functools.partial(up_kernel, len(pieces)),
        grid=(pairs,),
        in_specs=[pl.BlockSpec((slots, hidden_width), lambda i: (0, 0))] + specs(0) + specs(1),
        out_specs=[pl.BlockSpec((width, hidden_width), lambda i: (i, 0))] * 2,
        out_shape=[
            jax.ShapeDtypeStruct((pairs * width, hidden_width), jnp.float32),
            jax.ShapeDtypeStruct((pairs * width, hidden_width), jnp.bfloat16),
        ],
        compiler_params=pltpu.CompilerParams(vmem_limit_bytes=VMEM),
        cost_estimate=cost(
            2 * slots * hidden_width * chips * width,
            2 * chips * width * slots + 3 * chips * width * hidden_width,
        ),
        name="up_step",
    )(grad_pre, *pieces, *pieces)
    kept = kept.reshape(pairs, width, hidden_width)
    return [kept[i] for i in range(pairs)], sent.reshape(pairs, width, hidden_width)


def pick(table, index):
    return lax.dynamic_index_in_dim(table, index, 0, keepdims=False)


def per_device(tokens, out_grad, probs, routes, saved_gate, saved_up, down_weight):
    owners = lax.axis_size("expert")
    groups = lax.axis_size("dp")
    me = lax.axis_index("expert")
    group = lax.axis_index("dp")
    where = jnp.stack([me, group]).astype(jnp.int32)
    half = owners // 2
    chips = groups // 2
    tok_count, model_width = tokens.shape
    slot_rows, hidden_width = saved_gate.shape
    capacity = slot_rows // owners
    share = model_width // groups
    peers = list(range(0, half, 2))

    core = group % 2
    def columns(rows, block, lo, hi):
        return lax.dynamic_slice_in_dim(rows, block * share + lo, hi - lo, 1)

    def both_cores(rows, blocks, lo, hi):
        mine = jnp.concatenate([columns(rows, b, lo, hi) for b in blocks], axis=1)
        other = jnp.concatenate([columns(rows, b ^ 1, lo, hi) for b in blocks], axis=1)
        return jnp.concatenate([mine, swap(other, "dp", 1)], axis=0)

    blocks = [2 * r + core for r in range(chips)]
    per_part = chips // DY_PARTS
    dy_own = both_cores(out_grad, [2 * r + core for r in range(chips)], 0, share)
    dy_parts = [
        dy_own[:, h * per_part * share : (h + 1) * per_part * share] for h in range(DY_PARTS)
    ]

    owner_ids = jnp.arange(owners, dtype=jnp.int32) * EXP_DEV
    named = routes.T[None, :, :] == owner_ids[:, None, None]
    table_own = jnp.sum(jnp.where(named, probs.T[None, :, :].astype(jnp.float32), 0.0), axis=1)
    tables_core = jnp.stack([table_own, swap(table_own, "dp", 1)])
    tables_next = swap(after(tables_core, dy_parts[0]), "expert", 1)
    tables_near = jnp.concatenate([tables_core, tables_next])
    tables_far = swap(tables_near, "expert", half)

    peers = list(range(0, half, 2))
    same = lambda i: i

    def spread(sent):
        return [sent[0]] + [swap(sent[n], "expert", peers[n]) for n in range(1, len(peers))]

    def place_rows(choices, rows, steps=None, width=None, index=same):
        width = width or share
        steps = steps or rows[0].shape[1] // width
        return place(choices, rows, index, steps, width, peers, capacity)

    scaled_near, plain_near = choose(where, tables_near, peers, capacity)

    dy_next = swap(after(dy_own, tables_next), "expert", 1)
    dy_far0 = swap(dy_parts[0], "expert", half)
    dy_from_own = place_rows([(scaled_near, 0)], [dy_own])
    placed = dy_from_own[0]
    dy_from_own = spread(dy_from_own)
    dy_next, dy_far0, dy_from_own, tables_far, dy1 = lax.optimization_barrier(
        (dy_next, dy_far0, dy_from_own, tables_far, dy_parts[1])
    )

    dy_far1 = swap(dy1, "expert", half)
    dy_from_next = spread(place_rows([(scaled_near, 1)], [dy_next]))
    dy_far_next0 = swap(dy_far0, "expert", 1)
    x_own = both_cores(after(tokens, placed), [group ^ (2 * r) for r in range(chips)], 0, share)
    part_width = share // X_PARTS
    x_parts = [
        jnp.concatenate(
            [
                x_own[:, r * share + p * part_width : r * share + (p + 1) * part_width]
                for r in range(chips)
            ],
            axis=1,
        )
        for p in range(X_PARTS)
    ]
    order = me ^ jnp.arange(owners, dtype=jnp.int32)
    saved = jnp.stack([after(saved_gate, placed), saved_up]).reshape(2, owners, capacity, hidden_width)[:, order]
    scaled_far, plain_far = choose(where, after(tables_far, dy_from_next[0]), peers, capacity)
    dy_far1, dy_from_next, dy_far_next0, x_parts, saved, scaled_far = lax.optimization_barrier(
        (dy_far1, dy_from_next, dy_far_next0, x_parts, saved, scaled_far)
    )
    dy_near = [piece for pair in zip(dy_from_own, dy_from_next) for piece in pair]

    x_far0 = swap(x_parts[0], "expert", half)
    dy_spread0 = spread(place_rows([(scaled_far, 0), (scaled_far, 1)], [dy_far0, dy_far_next0]))
    dy_far_next1 = swap(dy_far1, "expert", 1)
    x_next0 = swap(x_parts[0], "expert", 1)
    saved = jnp.stack([after(saved, dy_far_next1), swap(saved, "dp", 1)], axis=2)
    saved = saved.reshape(2, 2 * slot_rows, hidden_width).astype(jnp.float32)
    gate_act = jax.nn.silu(saved[0])
    hidden = (gate_act * saved[1]).astype(jnp.bfloat16)
    block = hidden_width // groups
    hidden_t = hidden.T.reshape(groups, block, 2 * slot_rows)
    rows_order = [m for m in range(groups) if not m & 2] + [m for m in range(groups) if m & 2]
    hidden_t = jnp.concatenate([pick(hidden_t, group ^ m) for m in rows_order], axis=0)
    matrix = down_weight[0]
    x_far0, dy_spread0, dy_far_next1, x_next0, x_parts, hidden_t = lax.optimization_barrier(
        (x_far0, dy_spread0, dy_far_next1, x_next0, x_parts, hidden_t)
    )

    x_far1 = swap(x_parts[1], "expert", half)
    dy_spread1 = spread(place_rows([(scaled_far, 0), (scaled_far, 1)], [dy_far1, dy_far_next1]))
    x_far_next0 = swap(x_far0, "expert", 1)
    x_next1 = swap(x_parts[1], "expert", 1)
    held = after(dy_near[0], dy_spread1[0])
    terms = down_step(hidden_t, [held] + dy_near[1:], dy_spread0, chips // 2, share, 0)
    terms_kept = terms[0][0]
    down = [chip_sum(*terms)]
    x_far1, dy_spread1, x_far_next0, x_next1, terms_kept = lax.optimization_barrier(
        (x_far1, dy_spread1, x_far_next0, x_next1, terms_kept)
    )

    width = share // X_CHUNKS
    per = X_CHUNKS // X_PARTS
    plain = [(plain_near, 0), (plain_near, 1), (plain_far, 0), (plain_far, 1)]
    x_far_next1 = swap(x_far1, "expert", 1)
    rows = [x_parts[0], x_next0, x_far0, x_far_next0]
    x_spread0 = place_rows(plain, rows, chips, part_width)
    near = [after(dy_near[0], x_spread0[0], x_far_next1, down[0])] + dy_near[1:]
    x_spread0 = spread(x_spread0)
    terms = down_step(hidden_t, near, dy_spread1, chips // 2, share, per_part)
    near[0] = after(near[0], terms[0][0])
    raw = []
    down.append(chip_sum(*terms, raw))
    back = back_step(where, matrix, near, dy_spread0, share, 0, None)
    back = back_step(where, matrix, near, dy_spread1, share, per_part, back)
    back = back.reshape(owners, 2, capacity, hidden_width)
    other = [swap(back[:, 1 - g].astype(jnp.bfloat16), "dp", 1) for g in range(2)]
    x_rows = [x_parts[1], x_next1, x_far1]
    x_far_next1, x_spread0 = lax.optimization_barrier((x_far_next1, x_spread0))
    x_spread1 = place_rows(
        plain, x_rows + [x_far_next1], chips, part_width
    )
    other[0] = after(other[0], x_spread1[0], raw[-1])
    back = jnp.stack([back[:, g] + other[g].astype(jnp.float32) for g in range(2)], axis=1)
    back = back.reshape(2 * slot_rows, hidden_width)
    grad_pre = (back * gate_act).astype(jnp.bfloat16)
    slot_grad = jnp.sum(
        (hidden.astype(jnp.float32) * back).reshape(owners, 2, capacity, hidden_width)[:, 0], axis=2
    )

    up_terms = [up_step(grad_pre, x_spread0, n, per, chips) for n in range(per)]
    up_parts = [chip_sum(*terms) for terms in up_terms]
    grad_pre = after(grad_pre, up_terms[-1][1])
    bits = [1 << n for n in range(owners.bit_length() - 1)]
    near_bits = [bit for bit in bits if bit in (1, half)]
    far_bits = [bit for bit in bits if bit not in (1, half)]
    returned = exchange(after(slot_grad, up_terms[-1][1]), "expert", near_bits)
    x_spread1 = spread(x_spread1)
    for n in range(per):
        grad_pre = after(grad_pre, up_parts[n])
        up_terms.append(up_step(grad_pre, x_spread1, n, per, chips))
        grad_pre = after(grad_pre, up_terms[-1][1])
    up_parts += [chip_sum(*terms) for terms in up_terms[per:]]
    down_blocks = []
    for h in range(DY_PARTS):
        mine, other = down[h][:block], swap(after(down[h][block:], up_parts[0]), "dp", 1)
        for r in range(per_part):
            span = slice(r * share, (r + 1) * share)
            for c in range(2):
                down_blocks.append(jnp.where(core == c, mine[:, span], other[:, span]))
    down_share = jnp.concatenate(down_blocks, axis=1)
    returned = exchange(after(returned, up_terms[per][1]), "expert", far_bits)[order]
    position_own = slot_positions(table_own, capacity)
    chosen_own = (
        lax.broadcasted_iota(jnp.int32, (owners, capacity, tok_count), 1) == position_own[:, None, :]
    )
    token_grad = jnp.sum(jnp.where(chosen_own, returned[:, :, None], 0.0), axis=1)
    token_grad = jnp.where(
        position_own >= 0, token_grad / jnp.where(table_own > 0, table_own, 1.0), 0.0
    )
    prob_grad = jnp.sum(jnp.where(named, token_grad[:, None, :], 0.0), axis=0).T
    up_share = jnp.concatenate(up_parts, axis=0).astype(jnp.bfloat16)

    return down_share[None], up_share[None], prob_grad


def solution(mesh):
    in_specs = (
        P(("dp", "expert"), None),
        P(("dp", "expert"), None),
        P(("dp", "expert"), None),
        P(("dp", "expert"), None),
        P(("dp", "expert"), None),
        P(("dp", "expert"), None),
        P("expert", None, None),
    )
    out_specs = (P("expert", "dp", None), P("expert", "dp", None), P(("dp", "expert"), None))
    return jax.shard_map(
        per_device, mesh=mesh, in_specs=in_specs, out_specs=out_specs, check_vma=False
    )
```
